256 devices in a mesh: row: 8 (over y, core), col: 8 (over z), shot: 4 (over x).
Axes of the slice: x: 4, y: 4, z: 8, core: 2. Of those that a mesh axis runs over, the one named last changes fastest.
Arguments:
- right_side: float32 [256, 16, 512], P('shot', None, 'col'), may hold values from -6 to 6
- rest_solution: bfloat16 [256, 64, 512], P('shot', 'row', 'col'), may hold values from -6 to 6
- rest_basis: bfloat16 [64, 1024, 512], P('row'), may hold values from -0.25 to 0.25
- window_basis: bfloat16 [64, 64, 16, 512], P('row', None, None, 'col'), may hold values from -0.125 to 0.125
- ranks: int32 [64, 16], P('row'), may hold values from 1 to 64, as said below
- inverses: bfloat16 [16, 512, 512], P(None, ('row', 'col')), may hold values from -0.25 to 0.25
- child_map: int32 [2, 4096], replicated, may hold values from 0 to 8191, as said below
Outputs:
- solution: bfloat16 [256, 16, 512], P('shot', None, ('row', 'col'))
- child_values: bfloat16 [256, 2, 4096], P('shot', None, ('row', 'col'))
The draws below stay inside these ranges and needn't reach their ends.
Inputs may be any that keep to these rules, and one draw needn't show every extreme that they name: `ranks`: each tile's rank lies in 1 to 64, and some tile has rank 64. `child_map`: a window row index i * 512 + p; every window row is taken exactly once over both children. With G = 8 * 8 grid devices, grid device g = row index * 8 + col index holds the positions p with p // (512 // G) == g and the child rows q with q // (4096 // G) == g of each child; the child rows that device g holds take, from any one grid device, either none or exactly 4 window rows.
All inputs are finite; a program needn't handle non-finite values.
Results may differ from the reference program's by a relative error of at most 0.018.
Values may be sent and summed in bfloat16 or wider, within the bound.
A program may use at most 64 MiB of HBM per device.

```python
import jax
import jax.numpy as jnp

TILE = 512
WT = 16
RANK = 64
SOURCES = 256
REST_TILES = 64
CHILD_ROWS = 4096
PAIR_MOST = 4
N_ROW = 8
N_COL = 8


def draw_ranks(key, part):
    key = jax.random.fold_in(key, 11)
    first_key, second_key = jax.random.split(key)
    counted = REST_TILES * WT
    values = jax.random.randint(first_key, (counted,), 1, RANK + 1)
    chosen = jax.random.randint(second_key, (), 0, counted)
    values = jnp.where(jnp.arange(counted) == chosen, RANK, values)
    return values.reshape(REST_TILES, WT).astype(jnp.int32)


def draw_child_map(key, part):
    key = jax.random.fold_in(key, 23)
    grid_count = N_ROW * N_COL
    local_width = TILE // grid_count
    per_dest = WT * TILE // grid_count
    group_count = per_dest // PAIR_MOST
    child_count = CHILD_ROWS // grid_count
    order_key, sender_key, dest_key, offset_key, tie_key = jax.random.split(key, 5)
    row_keys = jax.random.split(order_key, grid_count)
    row_orders = jax.vmap(lambda one_key: jax.random.permutation(one_key, per_dest))(row_keys)
    senders = jnp.arange(grid_count, dtype=jnp.int32)[:, None]
    window_rows = row_orders // local_width * TILE + senders * local_width + row_orders % local_width
    sender_label = jax.random.permutation(sender_key, grid_count)
    dest_label = jax.random.permutation(dest_key, grid_count)
    offsets = jax.random.permutation(offset_key, grid_count)[:group_count]
    group_of = jnp.arange(per_dest, dtype=jnp.int32) // PAIR_MOST
    dests = dest_label[(sender_label[:, None] + offsets[group_of][None, :]) % grid_count]
    total = grid_count * per_dest
    tiebreak = jax.random.permutation(tie_key, total)
    scores = dests.reshape(total) * total + tiebreak
    ordering = jnp.argsort(scores, stable=True)
    ordered_rows = window_rows.reshape(total)[ordering]
    arranged = ordered_rows.reshape(grid_count, 2, child_count).transpose(1, 0, 2).reshape(2, CHILD_ROWS)
    return arranged.astype(jnp.int32)


def steps_of(stream_key, extent, cuts, low, largest):
    level, own = 1.0, jax.random.fold_in(stream_key, 6)
    for position, blocks in cuts:
        steps = jnp.exp(jax.random.uniform(jax.random.fold_in(own, position), (blocks,), jnp.float32, low / len(cuts), largest / len(cuts)))
        level = level * jnp.repeat(steps, extent[position] // blocks).reshape([-1 if axis == position else 1 for axis in range(len(extent))])
    return level


def noise(key, dims, deviation, bound, shards=(), kind=jnp.bfloat16):
    result = deviation * jax.random.normal(key, dims, jnp.float32)
    if shards:
        result = result * steps_of(key, dims, shards, -0.22, 0.18)
    return jnp.clip(result, -bound, bound).astype(kind)


def setup_inputs(seed: int = 0) -> dict:
    keys = jax.random.split(jax.random.key(seed), 8)
    return {
        "right_side": noise(keys[0], (SOURCES, WT, TILE), 1.0, 6.0, ((0, 4), (2, 8)), jnp.float32),
        "rest_solution": noise(keys[1], (SOURCES, REST_TILES, TILE), 1.0, 6.0, ((0, 4), (1, 8), (2, 8))),
        "rest_basis": noise(keys[2], (REST_TILES, WT * RANK, TILE), TILE ** -0.5, 0.25, ((0, 8),)),
        "window_basis": noise(keys[3], (REST_TILES, RANK, WT, TILE), (RANK * REST_TILES // 2) ** -0.5, 0.125, ((0, 8), (3, 8))),
        "ranks": draw_ranks(jax.random.fold_in(keys[7], 71), 0),
        "inverses": noise(keys[5], (WT, TILE, TILE), TILE ** -0.5, 0.25, ((1, 64),)),
        "child_map": draw_child_map(jax.random.fold_in(keys[7], 71), 0),
    }


def reference(right_side, rest_solution, rest_basis, window_basis, ranks, inverses, child_map):
    coeffs = jnp.einsum("jap,sjp->jas", rest_basis.astype(jnp.float32), rest_solution.astype(jnp.float32))
    coeffs = coeffs.reshape(REST_TILES, WT, RANK, SOURCES)
    rank_mask = jnp.arange(RANK, dtype=jnp.int32)[None, None, :] < ranks[:, :, None]
    masked = jnp.where(rank_mask[..., None], coeffs, jnp.float32(0.0)).astype(jnp.bfloat16)
    update = jnp.einsum("jkip,jiks->sip", window_basis.astype(jnp.float32), masked.astype(jnp.float32))
    reduced = (right_side - update).astype(jnp.bfloat16)
    solution = jnp.einsum("ipm,sim->sip", inverses.astype(jnp.float32), reduced.astype(jnp.float32)).astype(jnp.bfloat16)
    flat_rows = solution.reshape(SOURCES, WT * TILE)
    child_values = flat_rows[:, child_map.astype(jnp.int32)]
    return solution, child_values
```

```python
import jax
import jax.numpy as jnp
from jax import lax
from jax.experimental import pallas as pl
from jax.experimental.pallas import tpu as pltpu
from jax.sharding import PartitionSpec as P

MESH = pl.DeviceIdType.MESH
F32 = jnp.float32
BF16 = jnp.bfloat16
I32 = jnp.int32
N = 8


def iota(shape, axis):
    return lax.broadcasted_iota(I32, shape, axis)


def dot(a, b):
    return jnp.dot(a, b, preferred_element_type=F32)


def dot_tn(a, b):
    return lax.dot_general(a, b, (((0,), (0,)), ((), ())), preferred_element_type=F32)


def swap(x):
    return pltpu.roll(x, 64, 1)


def kernel(
    right_ref, sol_ref, basis_ref, wb_ref, ranks_ref, inv_ref, map_ref,
    out_sol, out_child,
    sol_v, sol_f, right_v, right_f, basis_v, wb_v, map_v, ranks_s,
    gath, w0, cm, msg, part, red, redg, invg, invl, solg, selm, s5, pk, chg,
    load_sem, basis_sem, ring_send, ring_recv, inv_send, inv_recv,
    p2_send, p2_recv, p3_send, p3_recv, p4_send, p4_recv, p5_send, p5_recv,
):
    r = lax.axis_index("row")
    c = lax.axis_index("col")
    right, left = lax.rem(c + 1, N), lax.rem(c + N - 1, N)

    def remote(src, dst, send, recv, axis, to):
        return pltpu.make_async_remote_copy(
            src_ref=src, dst_ref=dst, send_sem=send, recv_sem=recv,
            device_id={axis: to}, device_id_type=MESH,
        )

    load_sol = pltpu.make_async_copy(sol_ref, sol_v, load_sem.at[0])
    load_sol.start()
    load_wb = pltpu.make_async_copy(wb_ref, wb_v, load_sem.at[1])
    load_map = pltpu.make_async_copy(
        map_ref.at[:, pl.ds(pl.multiple_of(r * 512, 512), 512)], map_v, load_sem.at[2])
    load_ranks = pltpu.make_async_copy(ranks_ref, ranks_s, load_sem.at[3])
    load_right = pltpu.make_async_copy(
        right_ref.at[:, pl.ds(pl.multiple_of((r // 4) * 8, 8), 8), :], right_v, load_sem.at[4])
    load_inv = pltpu.make_async_copy(
        inv_ref.at[pl.ds(2 * r, 2)], invg.at[r], load_sem.at[5])

    barrier = pltpu.get_barrier_semaphore()
    for d in range(1, N):
        pl.semaphore_signal(barrier, inc=1, device_id={"col": lax.rem(c + d, N)}, device_id_type=MESH)
        pl.semaphore_signal(barrier, inc=1, device_id={"row": lax.rem(r + d, N)}, device_id_type=MESH)

    load_wb.start()
    load_map.start()
    load_ranks.start()
    load_right.start()
    load_inv.start()
    loads = [
        pltpu.make_async_copy(basis_ref.at[j], basis_v.at[j], basis_sem.at[j])
        for j in range(N)
    ]
    for load in loads:
        load.start()

    load_sol.wait()
    sol_f[...] = sol_v[...].astype(F32).reshape(512, 64)
    for jj in range(4):
        both = jnp.concatenate(
            [sol_f[pl.ds(2 * jj + h, 64, stride=8), :] for h in range(2)], axis=0)
        gath[jj, c] = both.T.astype(BF16)

    pl.semaphore_wait(barrier, 2 * (N - 1))

    def hop(jj, slot, to, way, step):
        return remote(gath.at[jj, slot], gath.at[jj, slot],
                      ring_send.at[way, step, jj], ring_recv.at[way, step, jj], "col", to)

    def slot_of(way, step):
        return lax.rem(c + (N - step if way == 0 else step), N)

    def ring_hop(step):
        for jj in range(4):
            for way in range(2):
                if step > 0:
                    hop(jj, slot_of(way, step), right, way, step - 1).wait_recv()
                if step < 3 or jj % 2 == way:
                    hop(jj, slot_of(way, step), (right, left)[way], way, step).start()

    ring_hop(0)
    for d in range(1, N):
        to = lax.rem(r + d, N)
        remote(inv_ref.at[pl.ds(2 * to, 2)], invg.at[r], inv_send.at[d], inv_recv.at[d], "row", to).start()

    load_wb.wait()
    row_i, col_i = iota((256, 256), 0), iota((256, 256), 1)
    perm = jnp.where(
        ((row_i >> 4) == (col_i & 15)) & ((row_i & 15) == (col_i >> 4)), 1.0, 0.0).astype(BF16)

    def regroup(step):
        jj, kb = step // 4, step % 4
        k0 = pl.multiple_of(kb * 16, 16)
        x = jnp.concatenate(
            [wb_v[2 * jj + h, pl.ds(k0, 16)].reshape(256, 64) for h in range(2)], axis=1)
        y = dot(perm, x).astype(BF16).reshape(16, 16, 128)
        w0[:, pl.ds(pl.multiple_of(jj * 64 + kb * 16, 16), 16), :] = y

    for step in range(8):
        regroup(step)
    ring_hop(1)
    for step in range(8, 16):
        regroup(step)
    ring_hop(2)

    low = iota((1, 128), 1) < 64
    load_map.wait()
    w = map_v[...]
    cc = (w >> 3) & 7
    code = (((w >> 9) & 1) << 9) + ((w >> 10) << 6) + (((w >> 6) & 7) << 3) + (w & 7) + 1
    mine = cc == c
    mine_f = jnp.where(mine, 1.0, 0.0)
    mine8 = jnp.where(iota((8, 512), 0) == 0, mine_f[0:1], mine_f[1:2]).astype(BF16)
    ta, tb = iota((512, 512), 0), iota((512, 512), 1)
    same = (ta >> 6) == (tb >> 6)
    before = dot(mine8, jnp.where(same & (ta < tb), 1.0, 0.0).astype(BF16))
    total = dot(mine8, jnp.where(same, 1.0, 0.0).astype(BF16))
    place = (before[0:1].astype(I32), (before[1:2] + total[0:1]).astype(I32))
    code_f = jnp.where(mine, code, 0).astype(F32)
    slots = []
    for g in range(4):
        at = slice(g * 128, (g + 1) * 128)
        ra, la = iota((64, 128), 0), iota((64, 128), 1)
        ours = (ra >> 5) == (la >> 6)
        acc = jnp.zeros((64, 128), F32)
        for ch in range(2):
            take = ours & ((ra & 31) == place[ch][:, at])
            acc = acc + jnp.where(take, code_f[ch:ch + 1, at], 0.0)
        slots.append(jnp.sum(acc, axis=1, keepdims=True))
    slot = jnp.concatenate(slots, axis=0).astype(I32)
    src = iota((256, 512), 1) + 1
    for h in range(2):
        selm[h * 256:(h + 1) * 256, :] = jnp.where(src + h * 512 == slot, 1.0, 0.0).astype(BF16)
    ra, la = iota((64, 512), 0), iota((64, 512), 1)
    selm[512:576, :] = jnp.where(
        la == ((ra >> 3) << 6) + r * 8 + (ra & 7), 1.0, 0.0).astype(BF16)

    x = map_v[:, pl.ds(pl.multiple_of((c // 2) * 128, 128), 128)]
    x_swapped = swap(x)
    odd = lax.rem(c, 2) == 1
    own = jnp.where(
        low, jnp.where(odd, x_swapped[0:1], x[0:1]), jnp.where(odd, x[1:2], x_swapped[1:2]))
    class_l = ((own >> 3) & 7).astype(F32)
    qa, qb = iota((128, 128), 0), iota((128, 128), 1)
    class_s = jnp.sum(jnp.where(qa == qb, class_l, 0.0), axis=1, keepdims=True)
    rank_s = jnp.sum(jnp.where((class_s == class_l) & (qb < qa), 1.0, 0.0), axis=1, keepdims=True)
    rank_i = rank_s.astype(I32)
    found = class_s.astype(I32) * 16 + (rank_i & 15)
    for h in range(2):
        s5[h] = jnp.where((qb == found) & ((rank_i >> 4) == h), 1.0, 0.0).astype(BF16)

    load_right.wait()
    right_f[...] = right_v[...].reshape(512, 64)
    base = 2 * lax.rem(r, 4)
    right_t = jnp.concatenate(
        [right_f[pl.ds(base + h, 64, stride=8), :] for h in range(2)], axis=0).T

    ring_hop(3)
    load_ranks.wait()

    k_of = iota((64, 128), 0)
    for jj in range(4):
        way = jj % 2
        hop(jj, slot_of(way, 4), right, way, 3).wait_recv()
        loads[2 * jj].wait()
        loads[2 * jj + 1].wait()
        g = gath[jj].reshape(512, 128)
        pair = [dot(basis_v[2 * jj + h], g) for h in range(2)]
        for i in range(16):
            at = slice(i * 64, (i + 1) * 64)
            limit = jnp.where(low, ranks_s[2 * jj, i], ranks_s[2 * jj + 1, i])
            both = jnp.where(low, pair[0][at], pair[1][at])
            cm[i, jj * 64:(jj + 1) * 64, :] = jnp.where(k_of < limit, both, 0.0).astype(BF16)

    def update(to):
        sums = []
        for h in range(2):
            u = dot_tn(w0[2 * to + h], cm[2 * to + h])
            sums.append(jnp.where(low, u[0:64], u[64:128]))
        return jnp.where(low, sums[0], sums[1]) + swap(jnp.where(low, sums[1], sums[0]))

    def p2(d, to):
        return remote(msg.at[d], part.at[d], p2_send.at[d], p2_recv.at[d], "row", to)

    for d in range(1, N):
        to = lax.rem(r + d, N)
        msg[d] = update(to).astype(BF16)
        p2(d, to).start()
    acc = right_t - update(r)

    load_inv.wait()
    for d in range(1, N):
        remote(inv_ref.at[pl.ds(2 * r, 2)], invg.at[r], inv_send.at[d], inv_recv.at[d], "row", r).wait_recv()
    for h in range(2):
        invl[h * 64:(h + 1) * 64, :] = invg[:, h].astype(F32).reshape(64, 512).astype(BF16)

    for d in range(1, N):
        p2(d, r).wait_recv()
        acc = acc - part[d].astype(F32)
    red[...] = acc.astype(BF16)
    redg[c] = acc.astype(BF16)

    def p3(d, to):
        return remote(red, redg.at[c], p3_send.at[d], p3_recv.at[d], "col", to)

    for d in range(1, N):
        p3(d, lax.rem(c + d, N)).start()
    for d in range(1, N):
        p3(d, c).wait_recv()

    s = dot(invl[...], redg[...].reshape(512, 128))
    solved = jnp.where(low, s[0:64], s[64:128]).astype(BF16)
    solg[r] = solved

    def p4(d, to):
        return remote(solg.at[r], solg.at[r], p4_send.at[d], p4_recv.at[d], "row", to)

    for d in range(1, N):
        p4(d, lax.rem(r + d, N)).start()
    for d in range(1, N):
        p4(d, r).wait_recv()

    picked = dot(selm[...], solg[...].reshape(512, 128))
    rows = jnp.where(low, picked[0:256], picked[256:512])
    rows = (rows + swap(rows)).reshape(8, 32, 128)
    pk[...] = jnp.where(low, rows[:, 0:16], rows[:, 16:32]).astype(BF16)
    chg[c] = pk[c]

    def p5(d, to):
        return remote(pk.at[to], chg.at[c], p5_send.at[d], p5_recv.at[d], "col", to)

    for d in range(1, N):
        p5(d, lax.rem(c + d, N)).start()

    own_rows = picked[512:576]
    out_sol[:, 0] = own_rows[:, 0:64].reshape(8, 8, 64).astype(BF16)
    out_sol[:, 1] = swap(own_rows)[:, 0:64].reshape(8, 8, 64).astype(BF16)

    for d in range(1, N):
        p5(d, c).wait_recv()
    got = chg[...].reshape(128, 128)
    child = jnp.where(low, dot(s5[0], got), dot(s5[1], got))
    child = child + swap(child)
    out_child[...] = child.T[0:64].astype(BF16)

    for jj in range(4):
        for step in range(4):
            for way in range(2):
                if step < 3 or jj % 2 == way:
                    hop(jj, c, right, way, step).wait_send()
    for d in range(1, N):
        remote(inv_ref.at[pl.ds(2 * r, 2)], invg.at[r], inv_send.at[d], inv_recv.at[d], "row", r).wait_send()
        p2(d, r).wait_send()
        p3(d, c).wait_send()
        p4(d, r).wait_send()
        p5(d, c).wait_send()


def on_device(right_side, rest_solution, rest_basis, window_basis, ranks, inverses, child_map):
    any_spec = pl.BlockSpec(memory_space=pl.ANY)
    vmem_spec = pl.BlockSpec(memory_space=pltpu.VMEM)
    dma = pltpu.SemaphoreType.DMA
    sol, child = pl.pallas_call(
        kernel,
        out_shape=(
            jax.ShapeDtypeStruct((8, 2, 8, 64), BF16),
            jax.ShapeDtypeStruct((64, 128), BF16),
        ),
        in_specs=[any_spec] * 7,
        out_specs=(vmem_spec, vmem_spec),
        scratch_shapes=[
            pltpu.VMEM((64, 8, 64), BF16),
            pltpu.VMEM((512, 64), F32),
            pltpu.VMEM((64, 8, 64), F32),
            pltpu.VMEM((512, 64), F32),
            pltpu.VMEM((8, 1024, 512), BF16),
            pltpu.VMEM((8, 64, 16, 64), BF16),
            pltpu.VMEM((2, 512), I32),
            pltpu.SMEM((8, 16), I32),
            pltpu.VMEM((4, 8, 64, 128), BF16),
            pltpu.VMEM((16, 256, 128), BF16),
            pltpu.VMEM((16, 256, 128), BF16),
            pltpu.VMEM((8, 64, 128), BF16),
            pltpu.VMEM((8, 64, 128), BF16),
            pltpu.VMEM((64, 128), BF16),
            pltpu.VMEM((8, 64, 128), BF16),
            pltpu.VMEM((8, 2, 8, 512), BF16),
            pltpu.VMEM((128, 512), BF16),
            pltpu.VMEM((8, 64, 128), BF16),
            pltpu.VMEM((576, 512), BF16),
            pltpu.VMEM((2, 128, 128), BF16),
            pltpu.VMEM((8, 16, 128), BF16),
            pltpu.VMEM((8, 16, 128), BF16),
            dma((6,)), dma((8,)), dma((2, 4, 4)), dma((2, 4, 4)),
            dma((8,)), dma((8,)),
            dma((8,)), dma((8,)), dma((8,)), dma((8,)),
            dma((8,)), dma((8,)), dma((8,)), dma((8,)),
        ],
        compiler_params=pltpu.CompilerParams(
            collective_id=0, has_side_effects=True, vmem_limit_bytes=56 * 1024 * 1024
        ),
        cost_estimate=pl.CostEstimate(flops=700_000_000, bytes_accessed=12_000_000, transcendentals=0),
    )(right_side, rest_solution, rest_basis, window_basis, ranks, inverses, child_map)
    solution_rows = sol.reshape(16, 8, 64).transpose(2, 0, 1)
    return solution_rows, child.reshape(64, 2, 64)


def solution(mesh):
    in_specs = (
        P("shot", None, "col"),
        P("shot", "row", "col"),
        P("row", None, None),
        P("row", None, None, "col"),
        P("row", None),
        P(None, ("row", "col"), None),
        P(),
    )
    out_specs = (P("shot", None, ("row", "col")), P("shot", None, ("row", "col")))
    return jax.shard_map(
        on_device, mesh=mesh, in_specs=in_specs, out_specs=out_specs, check_vma=False
    )
```

```python
import jax
import jax.numpy as jnp
from jax import lax
from jax.experimental import pallas as pl
from jax.experimental.pallas import tpu as pltpu
from jax.sharding import PartitionSpec as P

MESH = pl.DeviceIdType.MESH
F32 = jnp.float32
BF16 = jnp.bfloat16
I32 = jnp.int32
N = 8
NEAR = (2, 6, 1, 7)
FAR_FIRST = (4, 3, 5, 2, 6, 1, 7)


def iota(shape, axis):
    return lax.broadcasted_iota(I32, shape, axis)


def dot(a, b):
    return jnp.dot(a, b, preferred_element_type=F32)


def swap(x):
    return pltpu.roll(x, 64, 1)


def kernel(
    right_ref, sol_ref, basis_ref, wb_ref, ranks_ref, inv_ref, map_ref,
    out_sol, out_child,
    sol_v, sol_f, right_v, right_f, basis_v, wb_v, map_v, ranks_s,
    gath, w0, wt, cm, msg, part, red, redg, invg, invl, solg, selm, s5, pk, chg,
    load_sem, basis_sem, ring_send, ring_recv, inv_send, inv_recv,
    p2_send, p2_recv, p3_send, p3_recv, p4_send, p4_recv, p5_send, p5_recv,
):
    r = lax.axis_index("row")
    c = lax.axis_index("col")

    def remote(src, dst, send, recv, at, axis, to):
        return pltpu.make_async_remote_copy(
            src_ref=src, dst_ref=dst, send_sem=send.at[at], recv_sem=recv.at[at],
            device_id={axis: to}, device_id_type=MESH,
        )

    def local(src, dst, sem, at):
        return pltpu.make_async_copy(src, dst, sem.at[at])

    load_sol = local(sol_ref, sol_v, load_sem, 0)
    load_sol.start()
    load_wb = local(wb_ref, wb_v, load_sem, 1)
    load_map = local(
        map_ref.at[:, pl.ds(pl.multiple_of(r * 512, 512), 512)], map_v, load_sem, 2)
    load_ranks = local(ranks_ref, ranks_s, load_sem, 3)
    load_right = local(
        right_ref.at[:, pl.ds(pl.multiple_of((r // 4) * 8, 8), 8), :], right_v, load_sem, 4)
    load_inv = local(
        inv_ref.at[pl.ds(2 * r, 2)], invg.at[r], load_sem, 5)

    barrier = pltpu.get_barrier_semaphore()
    for d in NEAR:
        pl.semaphore_signal(barrier, inc=1, device_id={"col": lax.rem(c + d, N)}, device_id_type=MESH)
    for d in FAR_FIRST:
        pl.semaphore_signal(barrier, inc=1, device_id={"row": lax.rem(r + d, N)}, device_id_type=MESH)

    load_wb.start()
    load_map.start()
    load_ranks.start()
    load_right.start()
    load_inv.start()
    loads = [
        local(basis_ref.at[j], basis_v.at[j], basis_sem, j)
        for j in range(N)
    ]
    for load in loads:
        load.start()

    load_sol.wait()
    sol_f[...] = sol_v[...].astype(F32).reshape(512, 64)
    for jj in range(4):
        both = jnp.concatenate(
            [sol_f[pl.ds(2 * jj + h, 64, stride=8), :] for h in range(2)], axis=0)
        gath[jj, c] = both.T.astype(BF16)

    pl.semaphore_wait(barrier, len(NEAR) + len(FAR_FIRST))

    def chunk(jj, slot, to, lane):
        slot, to = lax.rem(c + slot + N, N), lax.rem(c + to + N, N)
        return remote(gath.at[jj, slot], gath.at[jj, slot], ring_send, ring_recv, (lane, jj), "col", to)

    for jj in range(4):
        chunk(jj, 0, 2, 0).start()
        chunk(jj, 0, -2, 1).start()
    for jj in range(4):
        chunk(jj, 0, 1, 2).start()
        chunk(jj, 0, -1, 3).start()

    def relay(jj):
        chunk(jj, -2, 2, 0).wait_recv()
        if jj % 2 == 0:
            chunk(jj, -2, 2, 6).start()
        chunk(jj, -2, 1, 4).start()
        chunk(jj, 2, -2, 1).wait_recv()
        if jj % 2 == 1:
            chunk(jj, 2, -2, 6).start()
        chunk(jj, 2, -1, 5).start()

    for d in FAR_FIRST:
        to = lax.rem(r + d, N)
        remote(inv_ref.at[pl.ds(2 * to, 2)], invg.at[r], inv_send, inv_recv, d, "row", to).start()

    load_wb.wait()
    row_i, col_i = iota((256, 256), 0), iota((256, 256), 1)
    perm = jnp.where(
        ((row_i >> 4) == (col_i & 15)) & ((row_i & 15) == (col_i >> 4)), 1.0, 0.0).astype(BF16)

    def regroup(step):
        jj, kb = step // 4, step % 4
        k0 = pl.multiple_of(kb * 16, 16)
        x = jnp.concatenate(
            [wb_v[2 * jj + h, pl.ds(k0, 16)].reshape(256, 64) for h in range(2)], axis=1)
        y = dot(perm, x).astype(BF16).reshape(16, 16, 128)
        w0[:, pl.ds(pl.multiple_of(jj * 64 + kb * 16, 16), 16), :] = y

    for step in range(16):
        regroup(step)
    for jj in range(4):
        relay(jj)
    for i in range(16):
        wt[i] = w0[i].T

    low = iota((1, 128), 1) < 64
    load_map.wait()
    w = map_v[...]
    cc = (w >> 3) & 7
    code = (((w >> 9) & 1) << 9) + ((w >> 10) << 6) + (((w >> 6) & 7) << 3) + (w & 7) + 1
    mine = cc == c
    mine_f = jnp.where(mine, 1.0, 0.0)
    mine8 = jnp.where(iota((8, 512), 0) == 0, mine_f[0:1], mine_f[1:2]).astype(BF16)
    ta, tb = iota((512, 512), 0), iota((512, 512), 1)
    same = (ta >> 6) == (tb >> 6)
    before = dot(mine8, jnp.where(same & (ta < tb), 1.0, 0.0).astype(BF16))
    total = dot(mine8, jnp.where(same, 1.0, 0.0).astype(BF16))
    place = (before[0:1].astype(I32), (before[1:2] + total[0:1]).astype(I32))
    code_f = jnp.where(mine, code, 0).astype(F32)
    slots = []
    for g in range(4):
        at = slice(g * 128, (g + 1) * 128)
        ra, la = iota((64, 128), 0), iota((64, 128), 1)
        ours = (ra >> 5) == (la >> 6)
        acc = jnp.zeros((64, 128), F32)
        for ch in range(2):
            take = ours & ((ra & 31) == place[ch][:, at])
            acc = acc + jnp.where(take, code_f[ch:ch + 1, at], 0.0)
        slots.append(jnp.sum(acc, axis=1, keepdims=True))
    slot = jnp.concatenate(slots, axis=0).astype(I32)
    src = iota((256, 512), 1) + 1
    for h in range(2):
        selm[h * 256:(h + 1) * 256, :] = jnp.where(src + h * 512 == slot, 1.0, 0.0).astype(BF16)
    ra, la = iota((64, 512), 0), iota((64, 512), 1)
    selm[512:576, :] = jnp.where(
        la == ((ra >> 3) << 6) + r * 8 + (ra & 7), 1.0, 0.0).astype(BF16)

    x = map_v[:, pl.ds(pl.multiple_of((c // 2) * 128, 128), 128)]
    x_swapped = swap(x)
    odd = lax.rem(c, 2) == 1
    own = jnp.where(
        low, jnp.where(odd, x_swapped[0:1], x[0:1]), jnp.where(odd, x[1:2], x_swapped[1:2]))
    class_l = ((own >> 3) & 7).astype(F32)
    qa, qb = iota((128, 128), 0), iota((128, 128), 1)
    class_s = jnp.sum(jnp.where(qa == qb, class_l, 0.0), axis=1, keepdims=True)
    rank_s = jnp.sum(jnp.where((class_s == class_l) & (qb < qa), 1.0, 0.0), axis=1, keepdims=True)
    rank_i = rank_s.astype(I32)
    found = class_s.astype(I32) * 16 + (rank_i & 15)
    for h in range(2):
        s5[h] = jnp.where((qb == found) & ((rank_i >> 4) == h), 1.0, 0.0).astype(BF16)

    load_right.wait()
    right_f[...] = right_v[...].reshape(512, 64)
    base = 2 * lax.rem(r, 4)
    right_t = jnp.concatenate(
        [right_f[pl.ds(base + h, 64, stride=8), :] for h in range(2)], axis=0).T

    load_ranks.wait()

    k_of = iota((64, 128), 0)
    for jj in range(4):
        for lane in (2, 3, 4, 5, 6):
            chunk(jj, 0, 1, lane).wait_recv()
        loads[2 * jj].wait()
        loads[2 * jj + 1].wait()
        g = gath[jj].reshape(512, 128)
        pair = [dot(basis_v[2 * jj + h], g) for h in range(2)]
        for i in range(16):
            at = slice(i * 64, (i + 1) * 64)
            limit = jnp.where(low, ranks_s[2 * jj, i], ranks_s[2 * jj + 1, i])
            both = jnp.where(low, pair[0][at], pair[1][at])
            cm[i, jj * 64:(jj + 1) * 64, :] = jnp.where(k_of < limit, both, 0.0).astype(BF16)

    def update(to):
        sums = []
        for h in range(2):
            u = dot(wt[2 * to + h], cm[2 * to + h])
            sums.append(jnp.where(low, u[0:64], u[64:128]))
        return jnp.where(low, sums[0], sums[1]) + swap(jnp.where(low, sums[1], sums[0]))

    def p2(d, to):
        return remote(msg.at[d], part.at[d], p2_send, p2_recv, d, "row", to)

    for batch in (FAR_FIRST[:4], FAR_FIRST[4:]):
        for d in batch:
            msg[d] = update(lax.rem(r + d, N)).astype(BF16)
        for d in batch:
            p2(d, lax.rem(r + d, N)).start()
    acc = right_t - update(r)

    load_inv.wait()
    for d in range(1, N):
        remote(inv_ref.at[pl.ds(2 * r, 2)], invg.at[r], inv_send, inv_recv, d, "row", r).wait_recv()
    for h in range(2):
        invl[h * 64:(h + 1) * 64, :] = invg[:, h].astype(F32).reshape(64, 512).astype(BF16)

    for d in range(1, N):
        p2(d, r).wait_recv()
        acc = acc - part[d].astype(F32)
    red[...] = acc.astype(BF16)
    redg[c] = acc.astype(BF16)

    def p3(d, to):
        return remote(red, redg.at[c], p3_send, p3_recv, d, "col", to)

    for d in FAR_FIRST:
        p3(d, lax.rem(c + d, N)).start()
    for d in range(1, N):
        p3(d, c).wait_recv()

    s = dot(invl[...], redg[...].reshape(512, 128))
    solved = jnp.where(low, s[0:64], s[64:128]).astype(BF16)
    solg[r] = solved

    def p4(d, to):
        return remote(solg.at[r], solg.at[r], p4_send, p4_recv, d, "row", to)

    for d in FAR_FIRST:
        p4(d, lax.rem(r + d, N)).start()
    for d in range(1, N):
        p4(d, r).wait_recv()

    picked = dot(selm[...], solg[...].reshape(512, 128))
    rows = jnp.where(low, picked[0:256], picked[256:512])
    rows = (rows + swap(rows)).reshape(8, 32, 128)
    pk[...] = jnp.where(low, rows[:, 0:16], rows[:, 16:32]).astype(BF16)
    chg[c] = pk[c]

    def p5(d, to):
        return remote(pk.at[to], chg.at[c], p5_send, p5_recv, d, "col", to)

    for d in FAR_FIRST:
        p5(d, lax.rem(c + d, N)).start()

    own_rows = picked[512:576]
    out_sol[:, 0] = own_rows[:, 0:64].reshape(8, 8, 64).astype(BF16)
    out_sol[:, 1] = swap(own_rows)[:, 0:64].reshape(8, 8, 64).astype(BF16)

    for d in range(1, N):
        p5(d, c).wait_recv()
    got = chg[...].reshape(128, 128)
    child = jnp.where(low, dot(s5[0], got), dot(s5[1], got))
    child = child + swap(child)
    out_child[...] = child.T[0:64].astype(BF16)

    for jj in range(4):
        for lane in range(7):
            chunk(jj, 0, 1, lane).wait_send()
    for d in range(1, N):
        remote(inv_ref.at[pl.ds(2 * r, 2)], invg.at[r], inv_send, inv_recv, d, "row", r).wait_send()
        p2(d, r).wait_send()
        p3(d, c).wait_send()
        p4(d, r).wait_send()
        p5(d, c).wait_send()


def on_device(right_side, rest_solution, rest_basis, window_basis, ranks, inverses, child_map):
    any_spec = pl.BlockSpec(memory_space=pl.ANY)
    vmem_spec = pl.BlockSpec(memory_space=pltpu.VMEM)
    dma = pltpu.SemaphoreType.DMA
    sol, child = pl.pallas_call(
        kernel,
        out_shape=(
            pltpu.VMEM((8, 2, 8, 64), BF16),
            pltpu.VMEM((64, 128), BF16),
        ),
        in_specs=[any_spec] * 7,
        out_specs=(vmem_spec, vmem_spec),
        scratch_shapes=[
            pltpu.VMEM((64, 8, 64), BF16),
            pltpu.VMEM((512, 64), F32),
            pltpu.VMEM((64, 8, 64), F32),
            pltpu.VMEM((512, 64), F32),
            pltpu.VMEM((8, 1024, 512), BF16),
            pltpu.VMEM((8, 64, 16, 64), BF16),
            pltpu.VMEM((2, 512), I32),
            pltpu.SMEM((8, 16), I32),
            pltpu.VMEM((4, 8, 64, 128), BF16),
            pltpu.VMEM((16, 256, 128), BF16),
            pltpu.VMEM((16, 128, 256), BF16),
            pltpu.VMEM((16, 256, 128), BF16),
            pltpu.VMEM((8, 64, 128), BF16),
            pltpu.VMEM((8, 64, 128), BF16),
            pltpu.VMEM((64, 128), BF16),
            pltpu.VMEM((8, 64, 128), BF16),
            pltpu.VMEM((8, 2, 8, 512), BF16),
            pltpu.VMEM((128, 512), BF16),
            pltpu.VMEM((8, 64, 128), BF16),
            pltpu.VMEM((576, 512), BF16),
            pltpu.VMEM((2, 128, 128), BF16),
            pltpu.VMEM((8, 16, 128), BF16),
            pltpu.VMEM((8, 16, 128), BF16),
            dma((6,)), dma((8,)), dma((7, 4)), dma((7, 4)),
            dma((8,)), dma((8,)),
            dma((8,)), dma((8,)), dma((8,)), dma((8,)),
            dma((8,)), dma((8,)), dma((8,)), dma((8,)),
        ],
        compiler_params=pltpu.CompilerParams(
            collective_id=0, has_side_effects=True, vmem_limit_bytes=56 * 1024 * 1024
        ),
        cost_estimate=pl.CostEstimate(flops=700_000_000, bytes_accessed=12_000_000, transcendentals=0),
    )(right_side, rest_solution, rest_basis, window_basis, ranks, inverses, child_map)
    solution_rows = sol.reshape(16, 8, 64).transpose(2, 0, 1)
    return solution_rows, child.reshape(64, 2, 64)


def solution(mesh):
    in_specs = (
        P("shot", None, "col"),
        P("shot", "row", "col"),
        P("row", None, None),
        P("row", None, None, "col"),
        P("row", None),
        P(None, ("row", "col"), None),
        P(),
    )
    out_specs = (P("shot", None, ("row", "col")), P("shot", None, ("row", "col")))
    return jax.shard_map(
        on_device, mesh=mesh, in_specs=in_specs, out_specs=out_specs, check_vma=False
    )
```

```python
import jax
import jax.numpy as jnp
from jax import lax
from jax.experimental import pallas as pl
from jax.experimental.pallas import tpu as pltpu
from jax.sharding import PartitionSpec as P

MESH = pl.DeviceIdType.MESH
F32 = jnp.float32
BF16 = jnp.bfloat16
I32 = jnp.int32
N = 8
NEAR = (2, 6, 1, 7)
FAR_FIRST = (4, 3, 5, 2, 6, 1, 7)


def iota(shape, axis):
    return lax.broadcasted_iota(I32, shape, axis)


def dot(a, b):
    return jnp.dot(a, b, preferred_element_type=F32)


def swap(x):
    return pltpu.roll(x, 64, 1)


def kernel(
    right_ref, sol_ref, basis_ref, wb_ref, ranks_ref, inv_ref, map_ref,
    out_sol, out_child,
    sol_v, sol_f, right_v, right_f, basis_v, wb_v, map_v, ranks_s,
    gath, w0, wt, cm, msg, part, red, redg, invg, invz, solv, selm, out_msg, fin,
    load_sem, basis_sem, ring_send, ring_recv, inv_send, inv_recv,
    p2_send, p2_recv, p3_send, p3_recv, p4_send, p4_recv, tile_send, tile_recv,
):
    r = lax.axis_index("row")
    c = lax.axis_index("col")

    def remote(src, dst, send, recv, at, axis, to):
        return pltpu.make_async_remote_copy(
            src_ref=src, dst_ref=dst, send_sem=send.at[at], recv_sem=recv.at[at],
            device_id={axis: to}, device_id_type=MESH,
        )

    def local(src, dst, sem, at):
        return pltpu.make_async_copy(src, dst, sem.at[at])

    load_sol = local(sol_ref, sol_v, load_sem, 0)
    load_sol.start()
    load_wb = local(wb_ref, wb_v, load_sem, 1)
    load_map = local(map_ref, map_v, load_sem, 2)
    load_ranks = local(ranks_ref, ranks_s, load_sem, 3)
    load_right = local(
        right_ref.at[:, pl.ds(pl.multiple_of((r // 4) * 8, 8), 8), :], right_v, load_sem, 4)
    load_inv = local(
        inv_ref.at[pl.ds(2 * r, 2)], invg.at[r], load_sem, 5)

    barrier = pltpu.get_barrier_semaphore()
    for d in NEAR:
        pl.semaphore_signal(barrier, inc=1, device_id={"col": lax.rem(c + d, N)}, device_id_type=MESH)
    for d in FAR_FIRST:
        pl.semaphore_signal(barrier, inc=1, device_id={"row": lax.rem(r + d, N)}, device_id_type=MESH)

    load_wb.start()
    load_map.start()
    load_ranks.start()
    load_right.start()
    load_inv.start()
    loads = [
        local(basis_ref.at[j], basis_v.at[j], basis_sem, j)
        for j in range(N)
    ]
    for load in loads:
        load.start()

    load_sol.wait()
    sol_f[...] = sol_v[...].astype(F32).reshape(512, 64)
    for jj in range(4):
        both = jnp.concatenate(
            [sol_f[pl.ds(2 * jj + h, 64, stride=8), :] for h in range(2)], axis=0)
        gath[jj, c] = both.T.astype(BF16)

    pl.semaphore_wait(barrier, len(NEAR) + len(FAR_FIRST))

    def chunk(jj, slot, to, lane):
        slot, to = lax.rem(c + slot + N, N), lax.rem(c + to + N, N)
        return remote(gath.at[jj, slot], gath.at[jj, slot], ring_send, ring_recv, (lane, jj), "col", to)

    for jj in range(4):
        chunk(jj, 0, 2, 0).start()
        chunk(jj, 0, -2, 1).start()
    for jj in range(4):
        chunk(jj, 0, 1, 2).start()
        chunk(jj, 0, -1, 3).start()

    def relay(jj):
        chunk(jj, -2, 2, 0).wait_recv()
        if jj % 2 == 0:
            chunk(jj, -2, 2, 6).start()
        chunk(jj, -2, 1, 4).start()
        chunk(jj, 2, -2, 1).wait_recv()
        if jj % 2 == 1:
            chunk(jj, 2, -2, 6).start()
        chunk(jj, 2, -1, 5).start()

    for d in FAR_FIRST:
        to = lax.rem(r + d, N)
        remote(inv_ref.at[pl.ds(2 * to, 2)], invg.at[r], inv_send, inv_recv, d, "row", to).start()

    load_wb.wait()
    row_i, col_i = iota((256, 256), 0), iota((256, 256), 1)
    perm = jnp.where(
        ((row_i >> 4) == (col_i & 15)) & ((row_i & 15) == (col_i >> 4)), 1.0, 0.0).astype(BF16)

    def regroup(step):
        jj, kb = step // 4, step % 4
        k0 = pl.multiple_of(kb * 16, 16)
        x = jnp.concatenate(
            [wb_v[2 * jj + h, pl.ds(k0, 16)].reshape(256, 64) for h in range(2)], axis=1)
        y = dot(perm, x).astype(BF16).reshape(16, 16, 128)
        w0[:, pl.ds(pl.multiple_of(jj * 64 + kb * 16, 16), 16), :] = y

    for step in range(16):
        regroup(step)
    for jj in range(4):
        relay(jj)
    for i in range(16):
        wt[i] = w0[i].T

    load_inv.wait()
    for d in range(1, N):
        remote(inv_ref.at[pl.ds(2 * r, 2)], invg.at[r], inv_send, inv_recv, d, "row", r).wait_recv()
    for h in range(2):
        invz[c, h] = invg[:, h].astype(F32).reshape(64, 512).astype(BF16)

    def tile_part(h, slot, to, lane):
        slot, to = lax.rem(c + slot + N, N), lax.rem(c + to + N, N)
        return remote(invz.at[slot, h], invz.at[slot, h], tile_send, tile_recv, (lane, h), "col", to)

    for h in range(2):
        tile_part(h, 0, 2, 0).start()
        tile_part(h, 0, -2, 1).start()
    for h in range(2):
        tile_part(h, 0, 1, 2).start()
        tile_part(h, 0, -1, 3).start()

    def tile_relay(h):
        tile_part(h, -2, 2, 0).wait_recv()
        tile_part(h, 2, -2, 1).wait_recv()
        if h == 0:
            tile_part(h, -2, 2, 6).start()
        else:
            tile_part(h, 2, -2, 6).start()
        tile_part(h, -2, 1, 4).start()
        tile_part(h, 2, -1, 5).start()

    low = iota((1, 128), 1) < 64
    load_map.wait()
    odd = lax.rem(c, 2) == 1
    own = []
    for to in range(N):
        x = map_v[:, pl.ds(pl.multiple_of((to * 4 + c // 2) * 128, 128), 128)]
        own.append(jnp.where(odd, swap(x), x))
    w = jnp.concatenate(own, axis=0)
    place = (((w >> 3) & 7) << 6) + (((w >> 6) & 7) << 3) + (w & 7)
    code = jnp.where((w >> 10) == r, place + (((w >> 9) & 1) << 9), -1)
    codes = jnp.concatenate([code.astype(F32), jnp.zeros((112, 128), F32)], axis=0).T.astype(I32)
    src = iota((64, 512), 1)
    for k in range(16):
        slot = codes[0:64, k:k + 1]
        for h in range(2):
            selm[h, k * 64:(k + 1) * 64, :] = jnp.where(src + h * 512 == slot, 1.0, 0.0).astype(BF16)

    load_right.wait()
    right_f[...] = right_v[...].reshape(512, 64)
    base = 2 * lax.rem(r, 4)
    right_t = jnp.concatenate(
        [right_f[pl.ds(base + h, 64, stride=8), :] for h in range(2)], axis=0).T

    load_ranks.wait()

    k_of = iota((64, 128), 0)
    for jj in range(4):
        for lane in (2, 3, 4, 5, 6):
            chunk(jj, 0, 1, lane).wait_recv()
        loads[2 * jj].wait()
        loads[2 * jj + 1].wait()
        g = gath[jj].reshape(512, 128)
        pair = [dot(basis_v[2 * jj + h], g) for h in range(2)]
        for i in range(16):
            at = slice(i * 64, (i + 1) * 64)
            limit = jnp.where(low, ranks_s[2 * jj, i], ranks_s[2 * jj + 1, i])
            both = jnp.where(low, pair[0][at], pair[1][at])
            cm[i, jj * 64:(jj + 1) * 64, :] = jnp.where(k_of < limit, both, 0.0).astype(BF16)

    def update(to):
        sums = []
        for h in range(2):
            u = dot(wt[2 * to + h], cm[2 * to + h])
            sums.append(jnp.where(low, u[0:64], u[64:128]))
        return jnp.where(low, sums[0], sums[1]) + swap(jnp.where(low, sums[1], sums[0]))

    def p2(d, to):
        return remote(msg.at[d], part.at[d], p2_send, p2_recv, d, "row", to)

    for batch in (FAR_FIRST[:4], FAR_FIRST[4:]):
        for d in batch:
            msg[d] = update(lax.rem(r + d, N)).astype(BF16)
        for d in batch:
            p2(d, lax.rem(r + d, N)).start()
    acc = right_t - update(r)

    for h in range(2):
        tile_relay(h)

    for d in range(1, N):
        p2(d, r).wait_recv()
        acc = acc - part[d].astype(F32)
    red[...] = acc.astype(BF16)
    redg[c] = acc.astype(BF16)

    def p3(d, to):
        return remote(red, redg.at[c], p3_send, p3_recv, d, "col", to)

    for d in FAR_FIRST:
        p3(d, lax.rem(c + d, N)).start()
    for d in range(1, N):
        p3(d, c).wait_recv()

    for h in range(2):
        for lane in (2, 3, 4, 5, 6):
            tile_part(h, 0, 1, lane).wait_recv()
    g = redg[...].reshape(512, 128)
    s = [dot(invz[:, h].reshape(512, 512), g) for h in range(2)]
    solved = jnp.where(low, s[0], s[1])
    solv[...] = solved
    solved = solved.astype(BF16)

    def p4(d, to):
        return remote(out_msg.at[to], fin.at[r], p4_send, p4_recv, d, "row", to)

    def pick(to):
        at = pl.ds(pl.multiple_of(to * 128, 128), 128)
        rows = jnp.where(low, dot(selm[0, at, :], solved), dot(selm[1, at, :], solved))
        rows = rows + swap(rows)
        out_msg[to, 0:64, :] = jnp.where(low, rows[0:64], rows[64:128]).astype(BF16)
        mine = solv[pl.ds(pl.multiple_of(c * 64 + to * 8, 8), 8), :]
        out_msg[to, 64:80, :] = jnp.concatenate([mine, mine], axis=0).astype(BF16)

    for batch in (FAR_FIRST[:4], FAR_FIRST[4:]):
        for d in batch:
            pick(lax.rem(r + d, N))
        for d in batch:
            p4(d, lax.rem(r + d, N)).start()
    pick(r)
    fin[r] = out_msg[r]
    for d in range(1, N):
        p4(d, r).wait_recv()

    child = jnp.zeros((64, 128), F32)
    for k in range(N):
        child = child + fin[k, 0:64, :].astype(F32)
        rows = fin[k, 64:80, :].astype(F32)
        out_sol[k, 0] = rows[0:8, 0:64].astype(BF16)
        out_sol[k, 1] = swap(rows)[0:8, 0:64].astype(BF16)
    child = child.T
    out_child[...] = jnp.concatenate([child[0:64], child[64:128]], axis=1).astype(BF16)

    for jj in range(4):
        for lane in range(7):
            chunk(jj, 0, 1, lane).wait_send()
    for d in range(1, N):
        remote(inv_ref.at[pl.ds(2 * r, 2)], invg.at[r], inv_send, inv_recv, d, "row", r).wait_send()
        p2(d, r).wait_send()
        p3(d, c).wait_send()
        p4(d, r).wait_send()
    for h in range(2):
        for lane in range(7):
            tile_part(h, 0, 1, lane).wait_send()


def on_device(right_side, rest_solution, rest_basis, window_basis, ranks, inverses, child_map):
    any_spec = pl.BlockSpec(memory_space=pl.ANY)
    vmem_spec = pl.BlockSpec(memory_space=pltpu.VMEM)
    dma = pltpu.SemaphoreType.DMA
    sol, child = pl.pallas_call(
        kernel,
        out_shape=(
            pltpu.VMEM((8, 2, 8, 64), BF16),
            pltpu.VMEM((64, 128), BF16),
        ),
        in_specs=[any_spec] * 7,
        out_specs=(vmem_spec, vmem_spec),
        scratch_shapes=[
            pltpu.VMEM((64, 8, 64), BF16),
            pltpu.VMEM((512, 64), F32),
            pltpu.VMEM((64, 8, 64), F32),
            pltpu.VMEM((512, 64), F32),
            pltpu.VMEM((8, 1024, 512), BF16),
            pltpu.VMEM((8, 64, 16, 64), BF16),
            pltpu.VMEM((2, 4096), I32),
            pltpu.SMEM((8, 16), I32),
            pltpu.VMEM((4, 8, 64, 128), BF16),
            pltpu.VMEM((16, 256, 128), BF16),
            pltpu.VMEM((16, 128, 256), BF16),
            pltpu.VMEM((16, 256, 128), BF16),
            pltpu.VMEM((8, 64, 128), BF16),
            pltpu.VMEM((8, 64, 128), BF16),
            pltpu.VMEM((64, 128), BF16),
            pltpu.VMEM((8, 64, 128), BF16),
            pltpu.VMEM((8, 2, 8, 512), BF16),
            pltpu.VMEM((8, 2, 64, 512), BF16),
            pltpu.VMEM((512, 128), F32),
            pltpu.VMEM((2, 1024, 512), BF16),
            pltpu.VMEM((8, 80, 128), BF16),
            pltpu.VMEM((8, 80, 128), BF16),
            dma((6,)), dma((8,)), dma((7, 4)), dma((7, 4)),
            dma((8,)), dma((8,)),
            dma((8,)), dma((8,)), dma((8,)), dma((8,)),
            dma((8,)), dma((8,)), dma((7, 2)), dma((7, 2)),
        ],
        compiler_params=pltpu.CompilerParams(
            collective_id=0, has_side_effects=True, vmem_limit_bytes=56 * 1024 * 1024
        ),
        cost_estimate=pl.CostEstimate(flops=700_000_000, bytes_accessed=12_000_000, transcendentals=0),
    )(right_side, rest_solution, rest_basis, window_basis, ranks, inverses, child_map)
    solution_rows = sol.reshape(16, 8, 64).transpose(2, 0, 1)
    return solution_rows, child.reshape(64, 2, 64)


def solution(mesh):
    in_specs = (
        P("shot", None, "col"),
        P("shot", "row", "col"),
        P("row", None, None),
        P("row", None, None, "col"),
        P("row", None),
        P(None, ("row", "col"), None),
        P(),
    )
    out_specs = (P("shot", None, ("row", "col")), P("shot", None, ("row", "col")))
    return jax.shard_map(
        on_device, mesh=mesh, in_specs=in_specs, out_specs=out_specs, check_vma=False
    )
```

```python
import jax
import jax.numpy as jnp
from jax import lax
from jax.experimental import pallas as pl
from jax.experimental.pallas import tpu as pltpu
from jax.sharding import PartitionSpec as P

MESH = pl.DeviceIdType.MESH
F32 = jnp.float32
BF16 = jnp.bfloat16
I32 = jnp.int32
N = 8
NEAR = (2, 6, 1, 7)
FAR_FIRST = (4, 3, 5, 2, 6, 1, 7)


def iota(shape, axis):
    return lax.broadcasted_iota(I32, shape, axis)


def dot(a, b):
    return jnp.dot(a, b, preferred_element_type=F32)


def swap(x):
    return pltpu.roll(x, 64, 1)


def kernel(
    right_ref, sol_ref, basis_ref, wb_ref, ranks_ref, inv_ref, map_ref,
    out_sol, out_child,
    sol_v, sol_f, right_v, right_f, basis_v, wb_v, map_v, ranks_s,
    gath, half, w0, wt, cm, msg, part, red, redg, invg, invl, solg, selm, s5, pk, chg,
    load_sem, basis_sem, ring_send, ring_recv, inv_send, inv_recv,
    p2_send, p2_recv, p3_send, p3_recv, p4_send, p4_recv, p5_send, p5_recv, ready,
):
    r = lax.axis_index("row")
    c = lax.axis_index("col")

    def remote(src, dst, send, recv, at, axis, to):
        return pltpu.make_async_remote_copy(
            src_ref=src, dst_ref=dst, send_sem=send.at[at], recv_sem=recv.at[at],
            device_id={axis: to}, device_id_type=MESH,
        )

    def local(src, dst, sem, at):
        return pltpu.make_async_copy(src, dst, sem.at[at])

    load_sol = local(sol_ref, sol_v, load_sem, 0)
    load_sol.start()
    load_wb = local(wb_ref, wb_v, load_sem, 1)
    load_map = local(
        map_ref.at[:, pl.ds(pl.multiple_of(r * 512, 512), 512)], map_v, load_sem, 2)
    load_ranks = local(ranks_ref, ranks_s, load_sem, 3)
    load_right = local(
        right_ref.at[:, pl.ds(pl.multiple_of((r // 4) * 8, 8), 8), :], right_v, load_sem, 4)
    load_inv = local(
        inv_ref.at[pl.ds(2 * r, 2)], invg.at[r], load_sem, 5)

    barrier = pltpu.get_barrier_semaphore()

    def lateness(axis, index):
        return jnp.minimum(index, N - index) if axis == "col" else jnp.minimum(index // 2, 4 - index // 2)

    peers = [("col", d) for d in NEAR] + [("row", d) for d in FAR_FIRST]
    later, awaited = {}, 0
    for axis, d in peers:
        me = c if axis == "col" else r
        to = lax.rem(me + d, N)
        mine, its = lateness(axis, me), lateness(axis, to)
        later[axis, d] = its > mine
        awaited = awaited + jnp.where(its > mine, 0, 1)

        @pl.when(its >= mine)
        def _(axis=axis, to=to):
            pl.semaphore_signal(barrier, inc=1, device_id={axis: to}, device_id_type=MESH)

    load_wb.start()
    load_map.start()
    load_ranks.start()
    load_right.start()
    load_inv.start()
    loads = [
        local(basis_ref.at[j], basis_v.at[j], basis_sem, j)
        for j in range(N)
    ]
    for load in loads:
        load.start()

    load_sol.wait()
    sol_f[...] = sol_v[...].astype(F32).reshape(512, 64)
    for jj in range(4):
        both = jnp.concatenate(
            [sol_f[pl.ds(2 * jj + h, 64, stride=8), :] for h in range(2)], axis=0)
        gath[jj, c] = both.T.astype(BF16)

    pl.semaphore_wait(barrier, awaited)
    for n, (axis, d) in enumerate(peers):
        me = c if axis == "col" else r
        to = lax.rem(me + d, N)

        @pl.when(lateness(axis, to) < lateness(axis, me))
        def _(axis=axis, d=d, to=to):
            pl.semaphore_signal(
                ready.at[peers.index((axis, N - d))], inc=1, device_id={axis: to}, device_id_type=MESH)

    def released(axis, d):
        @pl.when(later[axis, d])
        def _():
            pl.semaphore_wait(ready.at[peers.index((axis, d))], 1)

    def chunk(jj, slot, to, lane):
        slot, to = lax.rem(c + slot + N, N), lax.rem(c + to + N, N)
        return remote(gath.at[jj, slot], gath.at[jj, slot], ring_send, ring_recv, (lane, jj), "col", to)

    direct = ((2, 0), (-2, 1), (1, 2), (-1, 3))
    for to, lane in direct:
        @pl.when(jnp.logical_not(later["col", to % N]))
        def _(to=to, lane=lane):
            for jj in range(4):
                chunk(jj, 0, to, lane).start()

    for to, lane in direct:
        @pl.when(later["col", to % N])
        def _(to=to, lane=lane):
            pl.semaphore_wait(ready.at[peers.index(("col", to % N))], 1)
            for jj in range(4):
                chunk(jj, 0, to, lane).start()

    early = jnp.minimum(c, N - c) <= 1
    halved = (c == 2) | (c == 6)

    def relay(jj, side):
        chunk(jj, -2 * side, 2 * side, (1 - side) // 2).wait_recv()

        @pl.when(early | (halved if jj % 2 == (1 - side) // 2 else False))
        def _():
            chunk(jj, -2 * side, 2 * side, 6 + (1 - side) // 2).start()

        chunk(jj, -2 * side, side, 4 + (1 - side) // 2).start()

    load_wb.wait()
    row_i, col_i = iota((256, 256), 0), iota((256, 256), 1)
    perm = jnp.where(
        ((row_i >> 4) == (col_i & 15)) & ((row_i & 15) == (col_i >> 4)), 1.0, 0.0).astype(BF16)

    def regroup(step):
        jj, kb = step // 4, step % 4
        k0 = pl.multiple_of(kb * 16, 16)
        x = jnp.concatenate(
            [wb_v[2 * jj + h, pl.ds(k0, 16)].reshape(256, 64) for h in range(2)], axis=1)
        y = dot(perm, x).astype(BF16).reshape(16, 16, 128)
        w0[:, pl.ds(pl.multiple_of(jj * 64 + kb * 16, 16), 16), :] = y

    for step in range(16):
        regroup(step)
    for first in (1, -1):
        @pl.when((c < 4) if first == 1 else (c >= 4))
        def _(first=first):
            for side in (first, -first):
                for jj in range(4):
                    relay(jj, side)

    for d in FAR_FIRST:
        released("row", d)
        to = lax.rem(r + d, N)
        remote(inv_ref.at[pl.ds(2 * to, 2)], invg.at[r], inv_send, inv_recv, d, "row", to).start()

    low = iota((1, 128), 1) < 64

    def coeffs(jj, first):
        pairs = [lax.rem(first + k, 4) for k in range(2)]
        g = jnp.concatenate([gath[jj, pl.ds(2 * p, 2)].reshape(128, 128) for p in pairs], axis=0)
        both = []
        for h in range(2):
            cols = [pl.ds(pl.multiple_of(p * 128, 128), 128) for p in pairs]
            both.append(dot(jnp.concatenate([basis_v[2 * jj + h, :, at] for at in cols], axis=1), g))
        return jnp.where(low, both[0], both[1])

    near = lax.rem((c + 7) // 2, 4)
    for jj in range(4):
        chunk(jj, 0, 1, 2).wait_recv()
        chunk(jj, 0, 1, 3).wait_recv()
        loads[2 * jj].wait()
        loads[2 * jj + 1].wait()
        half[jj] = coeffs(jj, near)
    for i in range(16):
        wt[i] = w0[i].T
    load_ranks.wait()

    k_of = iota((64, 128), 0)
    for jj in range(4):
        over = jnp.where(lax.rem(c, 4) == 0, jj % 2, c // 4)
        for lane in (4, 5, 6 + over):
            chunk(jj, 0, 1, lane).wait_recv()
        total = half[jj] + coeffs(jj, lax.rem(near + 2, 4))
        for i in range(16):
            limit = jnp.where(low, ranks_s[2 * jj, i], ranks_s[2 * jj + 1, i])
            cut = jnp.where(k_of < limit, total[i * 64:(i + 1) * 64], 0.0)
            cm[i, jj * 64:(jj + 1) * 64, :] = cut.astype(BF16)

    def update(to):
        sums = []
        for h in range(2):
            u = dot(wt[2 * to + h], cm[2 * to + h])
            sums.append(jnp.where(low, u[0:64], u[64:128]))
        return jnp.where(low, sums[0], sums[1]) + swap(jnp.where(low, sums[1], sums[0]))

    def p2(d, to):
        return remote(msg.at[d], part.at[d], p2_send, p2_recv, d, "row", to)

    for batch in (FAR_FIRST[:4], FAR_FIRST[4:]):
        for d in batch:
            msg[d] = update(lax.rem(r + d, N)).astype(BF16)
        for d in batch:
            p2(d, lax.rem(r + d, N)).start()
    own_update = update(r)

    load_map.wait()
    w = map_v[...]
    cc = (w >> 3) & 7
    code = (((w >> 9) & 1) << 9) + ((w >> 10) << 6) + (((w >> 6) & 7) << 3) + (w & 7) + 1
    mine = cc == c
    mine_f = jnp.where(mine, 1.0, 0.0)
    mine8 = jnp.where(iota((8, 512), 0) == 0, mine_f[0:1], mine_f[1:2]).astype(BF16)
    ta, tb = iota((512, 512), 0), iota((512, 512), 1)
    same = (ta >> 6) == (tb >> 6)
    before = dot(mine8, jnp.where(same & (ta < tb), 1.0, 0.0).astype(BF16))
    total = dot(mine8, jnp.where(same, 1.0, 0.0).astype(BF16))
    place = (before[0:1].astype(I32), (before[1:2] + total[0:1]).astype(I32))
    code_f = jnp.where(mine, code, 0).astype(F32)
    slots = []
    for g in range(4):
        at = slice(g * 128, (g + 1) * 128)
        ra, la = iota((64, 128), 0), iota((64, 128), 1)
        ours = (ra >> 5) == (la >> 6)
        acc = jnp.zeros((64, 128), F32)
        for ch in range(2):
            take = ours & ((ra & 31) == place[ch][:, at])
            acc = acc + jnp.where(take, code_f[ch:ch + 1, at], 0.0)
        slots.append(jnp.sum(acc, axis=1, keepdims=True))
    slot = jnp.concatenate(slots, axis=0).astype(I32)
    src = iota((256, 512), 1) + 1
    for h in range(2):
        selm[h * 256:(h + 1) * 256, :] = jnp.where(src + h * 512 == slot, 1.0, 0.0).astype(BF16)
    ra, la = iota((64, 512), 0), iota((64, 512), 1)
    selm[512:576, :] = jnp.where(
        la == ((ra >> 3) << 6) + r * 8 + (ra & 7), 1.0, 0.0).astype(BF16)

    load_right.wait()
    right_f[...] = right_v[...].reshape(512, 64)
    base = 2 * lax.rem(r, 4)
    right_t = jnp.concatenate(
        [right_f[pl.ds(base + h, 64, stride=8), :] for h in range(2)], axis=0).T

    acc = right_t - own_update
    for d in range(1, N):
        p2(d, r).wait_recv()
        acc = acc - part[d].astype(F32)
    red[...] = acc.astype(BF16)
    redg[c] = acc.astype(BF16)

    def p3(d, to):
        return remote(red, redg.at[c], p3_send, p3_recv, d, "col", to)

    for d in FAR_FIRST:
        p3(d, lax.rem(c + d, N)).start()
    load_inv.wait()
    for d in range(1, N):
        remote(inv_ref.at[pl.ds(2 * r, 2)], invg.at[r], inv_send, inv_recv, d, "row", r).wait_recv()
    for h in range(2):
        invl[h * 64:(h + 1) * 64, :] = invg[:, h].astype(F32).reshape(64, 512).astype(BF16)

    x = map_v[:, pl.ds(pl.multiple_of((c // 2) * 128, 128), 128)]
    x_swapped = swap(x)
    odd = lax.rem(c, 2) == 1
    own = jnp.where(
        low, jnp.where(odd, x_swapped[0:1], x[0:1]), jnp.where(odd, x[1:2], x_swapped[1:2]))
    class_l = ((own >> 3) & 7).astype(F32)
    qa, qb = iota((128, 128), 0), iota((128, 128), 1)
    class_s = jnp.sum(jnp.where(qa == qb, class_l, 0.0), axis=1, keepdims=True)
    rank_s = jnp.sum(jnp.where((class_s == class_l) & (qb < qa), 1.0, 0.0), axis=1, keepdims=True)
    rank_i = rank_s.astype(I32)
    found = class_s.astype(I32) * 16 + (rank_i & 15)
    for h in range(2):
        s5[h] = jnp.where((qb == found) & ((rank_i >> 4) == h), 1.0, 0.0).astype(BF16)

    for d in range(1, N):
        p3(d, c).wait_recv()

    s = dot(invl[...], redg[...].reshape(512, 128))
    solved = jnp.where(low, s[0:64], s[64:128]).astype(BF16)
    solg[r] = solved

    def p4(d, to):
        return remote(solg.at[r], solg.at[r], p4_send, p4_recv, d, "row", to)

    for d in FAR_FIRST:
        p4(d, lax.rem(r + d, N)).start()
    for d in range(1, N):
        p4(d, r).wait_recv()

    picked = dot(selm[...], solg[...].reshape(512, 128))
    rows = jnp.where(low, picked[0:256], picked[256:512])
    rows = (rows + swap(rows)).reshape(8, 32, 128)
    pk[...] = jnp.where(low, rows[:, 0:16], rows[:, 16:32]).astype(BF16)
    chg[c] = pk[c]

    def p5(d, to):
        return remote(pk.at[to], chg.at[c], p5_send, p5_recv, d, "col", to)

    for d in FAR_FIRST:
        p5(d, lax.rem(c + d, N)).start()

    own_rows = picked[512:576]
    out_sol[:, 0] = own_rows[:, 0:64].reshape(8, 8, 64).astype(BF16)
    out_sol[:, 1] = swap(own_rows)[:, 0:64].reshape(8, 8, 64).astype(BF16)

    for d in range(1, N):
        p5(d, c).wait_recv()
    got = chg[...].reshape(128, 128)
    child = jnp.where(low, dot(s5[0], got), dot(s5[1], got))
    child = child + swap(child)
    out_child[...] = child.T[0:64].astype(BF16)

    for jj in range(4):
        for lane in range(6):
            chunk(jj, 0, 1, lane).wait_send()
        for lane in (6, 7):
            @pl.when(early | (halved if jj % 2 == lane - 6 else False))
            def _(jj=jj, lane=lane):
                chunk(jj, 0, 1, lane).wait_send()
    for d in range(1, N):
        remote(inv_ref.at[pl.ds(2 * r, 2)], invg.at[r], inv_send, inv_recv, d, "row", r).wait_send()
        p2(d, r).wait_send()
        p3(d, c).wait_send()
        p4(d, r).wait_send()
        p5(d, c).wait_send()


def on_device(right_side, rest_solution, rest_basis, window_basis, ranks, inverses, child_map):
    any_spec = pl.BlockSpec(memory_space=pl.ANY)
    vmem_spec = pl.BlockSpec(memory_space=pltpu.VMEM)
    dma = pltpu.SemaphoreType.DMA
    sol, child = pl.pallas_call(
        kernel,
        out_shape=(
            pltpu.VMEM((8, 2, 8, 64), BF16),
            pltpu.VMEM((64, 128), BF16),
        ),
        in_specs=[any_spec] * 7,
        out_specs=(vmem_spec, vmem_spec),
        scratch_shapes=[
            pltpu.VMEM((64, 8, 64), BF16),
            pltpu.VMEM((512, 64), F32),
            pltpu.VMEM((64, 8, 64), F32),
            pltpu.VMEM((512, 64), F32),
            pltpu.VMEM((8, 1024, 512), BF16),
            pltpu.VMEM((8, 64, 16, 64), BF16),
            pltpu.VMEM((2, 512), I32),
            pltpu.SMEM((8, 16), I32),
            pltpu.VMEM((4, 8, 64, 128), BF16),
            pltpu.VMEM((4, 1024, 128), F32),
            pltpu.VMEM((16, 256, 128), BF16),
            pltpu.VMEM((16, 128, 256), BF16),
            pltpu.VMEM((16, 256, 128), BF16),
            pltpu.VMEM((8, 64, 128), BF16),
            pltpu.VMEM((8, 64, 128), BF16),
            pltpu.VMEM((64, 128), BF16),
            pltpu.VMEM((8, 64, 128), BF16),
            pltpu.VMEM((8, 2, 8, 512), BF16),
            pltpu.VMEM((128, 512), BF16),
            pltpu.VMEM((8, 64, 128), BF16),
            pltpu.VMEM((576, 512), BF16),
            pltpu.VMEM((2, 128, 128), BF16),
            pltpu.VMEM((8, 16, 128), BF16),
            pltpu.VMEM((8, 16, 128), BF16),
            dma((6,)), dma((8,)), dma((8, 4)), dma((8, 4)),
            dma((8,)), dma((8,)),
            dma((8,)), dma((8,)), dma((8,)), dma((8,)),
            dma((8,)), dma((8,)), dma((8,)), dma((8,)),
            pltpu.SemaphoreType.REGULAR((len(NEAR) + len(FAR_FIRST),)),
        ],
        compiler_params=pltpu.CompilerParams(
            collective_id=0, has_side_effects=True, vmem_limit_bytes=56 * 1024 * 1024
        ),
        cost_estimate=pl.CostEstimate(flops=700_000_000, bytes_accessed=12_000_000, transcendentals=0),
    )(right_side, rest_solution, rest_basis, window_basis, ranks, inverses, child_map)
    solution_rows = sol.reshape(16, 8, 64).transpose(2, 0, 1)
    return solution_rows, child.reshape(64, 2, 64)


def solution(mesh):
    in_specs = (
        P("shot", None, "col"),
        P("shot", "row", "col"),
        P("row", None, None),
        P("row", None, None, "col"),
        P("row", None),
        P(None, ("row", "col"), None),
        P(),
    )
    out_specs = (P("shot", None, ("row", "col")), P("shot", None, ("row", "col")))
    return jax.shard_map(
        on_device, mesh=mesh, in_specs=in_specs, out_specs=out_specs, check_vma=False
    )
```

```python
import jax
import jax.numpy as jnp
from jax import lax
from jax.experimental import pallas as pl
from jax.experimental.pallas import tpu as pltpu
from jax.sharding import PartitionSpec as P

MESH = pl.DeviceIdType.MESH
F32 = jnp.float32
BF16 = jnp.bfloat16
I32 = jnp.int32
N = 8
NEAR = (2, 6, 1, 7)
FAR_FIRST = (4, 3, 5, 2, 6, 1, 7)


def iota(shape, axis):
    return lax.broadcasted_iota(I32, shape, axis)


def dot(a, b):
    return jnp.dot(a, b, preferred_element_type=F32)


def swap(x):
    return pltpu.roll(x, 64, 1)


def kernel(
    right_ref, sol_ref, basis_ref, wb_ref, ranks_ref, inv_ref, map_ref,
    out_sol, out_child,
    sol_v, sol_f, right_v, right_f, basis_v, wb_v, map_v, ranks_s,
    gath, half, w0, wt, cm, msg, part, red, redg, invg, invl, solg, selm, s5, pk, chg,
    load_sem, basis_sem, ring_send, ring_recv, inv_send, inv_recv,
    p2_send, p2_recv, p3_send, p3_recv, p4_send, p4_recv, p5_send, p5_recv,
):
    r = lax.axis_index("row")
    c = lax.axis_index("col")

    def remote(src, dst, send, recv, at, axis, to):
        return pltpu.make_async_remote_copy(
            src_ref=src, dst_ref=dst, send_sem=send.at[at], recv_sem=recv.at[at],
            device_id={axis: to}, device_id_type=MESH,
        )

    def local(src, dst, sem, at):
        return pltpu.make_async_copy(src, dst, sem.at[at])

    load_sol = local(sol_ref, sol_v, load_sem, 0)
    load_sol.start()
    load_wb = local(wb_ref, wb_v, load_sem, 1)
    load_map = local(
        map_ref.at[:, pl.ds(pl.multiple_of(r * 512, 512), 512)], map_v, load_sem, 2)
    load_ranks = local(ranks_ref, ranks_s, load_sem, 3)
    load_right = local(
        right_ref.at[:, pl.ds(pl.multiple_of((r // 4) * 8, 8), 8), :], right_v, load_sem, 4)
    load_inv = local(
        inv_ref.at[pl.ds(2 * r, 2)], invg.at[r], load_sem, 5)

    barrier = pltpu.get_barrier_semaphore()
    for d in NEAR:
        pl.semaphore_signal(barrier, inc=1, device_id={"col": lax.rem(c + d, N)}, device_id_type=MESH)
    for d in FAR_FIRST:
        pl.semaphore_signal(barrier, inc=1, device_id={"row": lax.rem(r + d, N)}, device_id_type=MESH)

    def loop(count, body):
        def step(n, carry):
            body(n)
            return carry

        lax.fori_loop(0, count, step, 0)

    def away(n):
        return 4 + (n + 1) // 2 * (1 - 2 * lax.rem(n, 2))

    load_wb.start()
    load_map.start()
    load_ranks.start()
    load_right.start()
    load_inv.start()
    def load_basis(j):
        return local(basis_ref.at[j], basis_v.at[j], basis_sem, j)

    loop(N, lambda j: load_basis(j).start())

    load_sol.wait()
    sol_f[...] = sol_v[...].astype(F32).reshape(512, 64)
    for jj in range(4):
        both = jnp.concatenate(
            [sol_f[pl.ds(2 * jj + h, 64, stride=8), :] for h in range(2)], axis=0)
        gath[jj, c] = both.T.astype(BF16)

    pl.semaphore_wait(barrier, len(NEAR) + len(FAR_FIRST))

    def chunk(jj, slot, to, lane):
        slot, to = lax.rem(c + slot + N, N), lax.rem(c + to + N, N)
        return remote(gath.at[jj, slot], gath.at[jj, slot], ring_send, ring_recv, (lane, jj), "col", to)

    def direct(jj):
        chunk(jj, 0, 2, 0).start()
        chunk(jj, 0, -2, 1).start()

    def next_to(jj):
        chunk(jj, 0, 1, 2).start()
        chunk(jj, 0, -1, 3).start()

    loop(4, direct)
    loop(4, next_to)

    def tile_rows(d, to):
        return remote(inv_ref.at[pl.ds(2 * to, 2)], invg.at[r], inv_send, inv_recv, d, "row", to)

    loop(N - 1, lambda n: tile_rows(away(n), lax.rem(r + away(n), N)).start())

    def relay(jj):
        way = 1 - 2 * lax.rem(jj, 2)
        for side in (1, -1):
            chunk(jj, -2 * side, 2 * side, (1 - side) // 2).wait_recv()

            @pl.when(way == side)
            def _(side=side):
                chunk(jj, -2 * side, 2 * side, 6).start()

            chunk(jj, -2 * side, side, 4 + (1 - side) // 2).start()

    load_wb.wait()
    row_i, col_i = iota((256, 256), 0), iota((256, 256), 1)
    perm = jnp.where(
        ((row_i >> 4) == (col_i & 15)) & ((row_i & 15) == (col_i >> 4)), 1.0, 0.0).astype(BF16)

    def regroup(step):
        jj, kb = step // 4, lax.rem(step, 4)
        k0 = pl.multiple_of(kb * 16, 16)
        x = jnp.concatenate(
            [wb_v[2 * jj + h, pl.ds(k0, 16)].reshape(256, 64) for h in range(2)], axis=1)
        y = dot(perm, x).astype(BF16).reshape(16, 16, 128)
        w0[:, pl.ds(pl.multiple_of(jj * 64 + kb * 16, 16), 16), :] = y

    loop(16, regroup)
    loop(4, relay)

    low = iota((1, 128), 1) < 64

    def coeffs(jj, first):
        pairs = [lax.rem(first + k, 4) for k in range(2)]
        g = jnp.concatenate([gath[jj, pl.ds(2 * p, 2)].reshape(128, 128) for p in pairs], axis=0)
        both = []
        for h in range(2):
            cols = [pl.ds(pl.multiple_of(p * 128, 128), 128) for p in pairs]
            both.append(dot(jnp.concatenate([basis_v[2 * jj + h, :, at] for at in cols], axis=1), g))
        return jnp.where(low, both[0], both[1])

    near = lax.rem((c + 7) // 2, 4)

    def near_half(jj):
        chunk(jj, 0, 1, 2).wait_recv()
        chunk(jj, 0, 1, 3).wait_recv()
        load_basis(2 * jj).wait()
        load_basis(2 * jj + 1).wait()
        half[jj] = coeffs(jj, near)

    loop(4, near_half)

    def turn(i):
        wt[i] = w0[i].T

    loop(16, turn)
    load_ranks.wait()
    k_of = iota((64, 128), 0)

    def far_half(jj):
        for lane in (4, 5, 6):
            chunk(jj, 0, 1, lane).wait_recv()
        total = half[jj] + coeffs(jj, lax.rem(near + 2, 4))
        for i in range(16):
            limit = jnp.where(low, ranks_s[2 * jj, i], ranks_s[2 * jj + 1, i])
            cut = jnp.where(k_of < limit, total[i * 64:(i + 1) * 64], 0.0)
            cm[i, pl.ds(pl.multiple_of(jj * 64, 64), 64), :] = cut.astype(BF16)

    loop(4, far_half)

    def update(to):
        sums = []
        for h in range(2):
            u = dot(wt[2 * to + h], cm[2 * to + h])
            sums.append(jnp.where(low, u[0:64], u[64:128]))
        return jnp.where(low, sums[0], sums[1]) + swap(jnp.where(low, sums[1], sums[0]))

    def p2(d, to):
        return remote(msg.at[d], part.at[d], p2_send, p2_recv, d, "row", to)

    def send_update(n):
        d = away(n)
        to = lax.rem(r + d, N)
        msg[d] = update(to).astype(BF16)
        p2(d, to).start()

    loop(N - 1, send_update)
    own_update = update(r)

    load_map.wait()
    w = map_v[...]
    cc = (w >> 3) & 7
    code = (((w >> 9) & 1) << 9) + ((w >> 10) << 6) + (((w >> 6) & 7) << 3) + (w & 7) + 1
    mine = cc == c
    mine_f = jnp.where(mine, 1.0, 0.0)
    mine8 = jnp.where(iota((8, 512), 0) == 0, mine_f[0:1], mine_f[1:2]).astype(BF16)
    ta, tb = iota((512, 512), 0), iota((512, 512), 1)
    same = (ta >> 6) == (tb >> 6)
    before = dot(mine8, jnp.where(same & (ta < tb), 1.0, 0.0).astype(BF16))
    total = dot(mine8, jnp.where(same, 1.0, 0.0).astype(BF16))
    place = (before[0:1].astype(I32), (before[1:2] + total[0:1]).astype(I32))
    code_f = jnp.where(mine, code, 0).astype(F32)
    slots = []
    for g in range(4):
        at = slice(g * 128, (g + 1) * 128)
        ra, la = iota((64, 128), 0), iota((64, 128), 1)
        ours = (ra >> 5) == (la >> 6)
        acc = jnp.zeros((64, 128), F32)
        for ch in range(2):
            take = ours & ((ra & 31) == place[ch][:, at])
            acc = acc + jnp.where(take, code_f[ch:ch + 1, at], 0.0)
        slots.append(jnp.sum(acc, axis=1, keepdims=True))
    slot = jnp.concatenate(slots, axis=0).astype(I32)
    src = iota((256, 512), 1) + 1
    for h in range(2):
        selm[h * 256:(h + 1) * 256, :] = jnp.where(src + h * 512 == slot, 1.0, 0.0).astype(BF16)
    ra, la = iota((64, 512), 0), iota((64, 512), 1)
    selm[512:576, :] = jnp.where(
        la == ((ra >> 3) << 6) + r * 8 + (ra & 7), 1.0, 0.0).astype(BF16)

    load_right.wait()
    right_f[...] = right_v[...].reshape(512, 64)
    base = 2 * lax.rem(r, 4)
    right_t = jnp.concatenate(
        [right_f[pl.ds(base + h, 64, stride=8), :] for h in range(2)], axis=0).T

    acc = right_t - own_update
    def less(n, acc):
        p2(n + 1, r).wait_recv()
        return acc - part[n + 1].astype(F32)

    acc = lax.fori_loop(0, N - 1, less, acc)
    red[...] = acc.astype(BF16)
    redg[c] = acc.astype(BF16)

    def p3(d, to):
        return remote(red, redg.at[c], p3_send, p3_recv, d, "col", to)

    loop(N - 1, lambda n: p3(away(n), lax.rem(c + away(n), N)).start())
    load_inv.wait()
    loop(N - 1, lambda n: tile_rows(n + 1, r).wait_recv())
    for h in range(2):
        invl[h * 64:(h + 1) * 64, :] = invg[:, h].astype(F32).reshape(64, 512).astype(BF16)

    x = map_v[:, pl.ds(pl.multiple_of((c // 2) * 128, 128), 128)]
    x_swapped = swap(x)
    odd = lax.rem(c, 2) == 1
    own = jnp.where(
        low, jnp.where(odd, x_swapped[0:1], x[0:1]), jnp.where(odd, x[1:2], x_swapped[1:2]))
    class_l = ((own >> 3) & 7).astype(F32)
    qa, qb = iota((128, 128), 0), iota((128, 128), 1)
    class_s = jnp.sum(jnp.where(qa == qb, class_l, 0.0), axis=1, keepdims=True)
    rank_s = jnp.sum(jnp.where((class_s == class_l) & (qb < qa), 1.0, 0.0), axis=1, keepdims=True)
    rank_i = rank_s.astype(I32)
    found = class_s.astype(I32) * 16 + (rank_i & 15)
    for h in range(2):
        s5[h] = jnp.where((qb == found) & ((rank_i >> 4) == h), 1.0, 0.0).astype(BF16)

    loop(N - 1, lambda n: p3(n + 1, c).wait_recv())

    s = dot(invl[...], redg[...].reshape(512, 128))
    solved = jnp.where(low, s[0:64], s[64:128]).astype(BF16)
    solg[r] = solved

    def p4(d, to):
        return remote(solg.at[r], solg.at[r], p4_send, p4_recv, d, "row", to)

    loop(N - 1, lambda n: p4(away(n), lax.rem(r + away(n), N)).start())
    loop(N - 1, lambda n: p4(n + 1, r).wait_recv())

    picked = dot(selm[...], solg[...].reshape(512, 128))
    rows = jnp.where(low, picked[0:256], picked[256:512])
    rows = (rows + swap(rows)).reshape(8, 32, 128)
    pk[...] = jnp.where(low, rows[:, 0:16], rows[:, 16:32]).astype(BF16)
    chg[c] = pk[c]

    def p5(d, to):
        return remote(pk.at[to], chg.at[c], p5_send, p5_recv, d, "col", to)

    loop(N - 1, lambda n: p5(away(n), lax.rem(c + away(n), N)).start())

    own_rows = picked[512:576]
    out_sol[:, 0] = own_rows[:, 0:64].reshape(8, 8, 64).astype(BF16)
    out_sol[:, 1] = swap(own_rows)[:, 0:64].reshape(8, 8, 64).astype(BF16)

    loop(N - 1, lambda n: p5(n + 1, c).wait_recv())
    got = chg[...].reshape(128, 128)
    child = jnp.where(low, dot(s5[0], got), dot(s5[1], got))
    child = child + swap(child)
    out_child[...] = child.T[0:64].astype(BF16)

    def sent(n):
        chunk(n // 7, 0, 1, lax.rem(n, 7)).wait_send()

    loop(28, sent)

    def sent_rows(n):
        tile_rows(n + 1, r).wait_send()
        p2(n + 1, r).wait_send()
        p3(n + 1, c).wait_send()
        p4(n + 1, r).wait_send()
        p5(n + 1, c).wait_send()

    loop(N - 1, sent_rows)


def on_device(right_side, rest_solution, rest_basis, window_basis, ranks, inverses, child_map):
    any_spec = pl.BlockSpec(memory_space=pl.ANY)
    vmem_spec = pl.BlockSpec(memory_space=pltpu.VMEM)
    dma = pltpu.SemaphoreType.DMA
    sol, child = pl.pallas_call(
        kernel,
        out_shape=(
            pltpu.VMEM((8, 2, 8, 64), BF16),
            pltpu.VMEM((64, 128), BF16),
        ),
        in_specs=[any_spec] * 7,
        out_specs=(vmem_spec, vmem_spec),
        scratch_shapes=[
            pltpu.VMEM((64, 8, 64), BF16),
            pltpu.VMEM((512, 64), F32),
            pltpu.VMEM((64, 8, 64), F32),
            pltpu.VMEM((512, 64), F32),
            pltpu.VMEM((8, 1024, 512), BF16),
            pltpu.VMEM((8, 64, 16, 64), BF16),
            pltpu.VMEM((2, 512), I32),
            pltpu.SMEM((8, 16), I32),
            pltpu.VMEM((4, 8, 64, 128), BF16),
            pltpu.VMEM((4, 1024, 128), F32),
            pltpu.VMEM((16, 256, 128), BF16),
            pltpu.VMEM((16, 128, 256), BF16),
            pltpu.VMEM((16, 256, 128), BF16),
            pltpu.VMEM((8, 64, 128), BF16),
            pltpu.VMEM((8, 64, 128), BF16),
            pltpu.VMEM((64, 128), BF16),
            pltpu.VMEM((8, 64, 128), BF16),
            pltpu.VMEM((8, 2, 8, 512), BF16),
            pltpu.VMEM((128, 512), BF16),
            pltpu.VMEM((8, 64, 128), BF16),
            pltpu.VMEM((576, 512), BF16),
            pltpu.VMEM((2, 128, 128), BF16),
            pltpu.VMEM((8, 16, 128), BF16),
            pltpu.VMEM((8, 16, 128), BF16),
            dma((6,)), dma((8,)), dma((7, 4)), dma((7, 4)),
            dma((8,)), dma((8,)),
            dma((8,)), dma((8,)), dma((8,)), dma((8,)),
            dma((8,)), dma((8,)), dma((8,)), dma((8,)),
        ],
        compiler_params=pltpu.CompilerParams(
            collective_id=0, has_side_effects=True, vmem_limit_bytes=56 * 1024 * 1024
        ),
        cost_estimate=pl.CostEstimate(flops=700_000_000, bytes_accessed=12_000_000, transcendentals=0),
    )(right_side, rest_solution, rest_basis, window_basis, ranks, inverses, child_map)
    solution_rows = sol.reshape(16, 8, 64).transpose(2, 0, 1)
    return solution_rows, child.reshape(64, 2, 64)


def solution(mesh):
    in_specs = (
        P("shot", None, "col"),
        P("shot", "row", "col"),
        P("row", None, None),
        P("row", None, None, "col"),
        P("row", None),
        P(None, ("row", "col"), None),
        P(),
    )
    out_specs = (P("shot", None, ("row", "col")), P("shot", None, ("row", "col")))
    return jax.shard_map(
        on_device, mesh=mesh, in_specs=in_specs, out_specs=out_specs, check_vma=False
    )
```

```python
import jax
import jax.numpy as jnp
from jax import lax
from jax.experimental import pallas as pl
from jax.experimental.pallas import tpu as pltpu
from jax.sharding import PartitionSpec as P

MESH = pl.DeviceIdType.MESH
F32 = jnp.float32
BF16 = jnp.bfloat16
I32 = jnp.int32
N = 8
NEAR = (2, 6, 1, 7)
FAR_FIRST = (4, 3, 5, 2, 6, 1, 7)


def iota(shape, axis):
    return lax.broadcasted_iota(I32, shape, axis)


def dot(a, b):
    return jnp.dot(a, b, preferred_element_type=F32)


def swap(x):
    return pltpu.roll(x, 64, 1)


def kernel(
    right_ref, sol_ref, basis_ref, wb_ref, ranks_ref, inv_ref, map_ref,
    out_sol, out_child,
    sol_v, sol_f, right_v, right_f, basis_v, wb_v, map_v, ranks_s,
    gath, half, w0, wt, cm, msg, part, red, redg, invg, invl, solg, selm, s5, pk, chg,
    load_sem, basis_sem, ring_send, ring_recv, inv_send, inv_recv,
    p2_send, p2_recv, p3_send, p3_recv, p4_send, p4_recv, p5_send, p5_recv,
):
    r = lax.axis_index("row")
    c = lax.axis_index("col")

    def remote(src, dst, send, recv, at, axis, to):
        return pltpu.make_async_remote_copy(
            src_ref=src, dst_ref=dst, send_sem=send.at[at], recv_sem=recv.at[at],
            device_id={axis: to}, device_id_type=MESH,
        )

    def local(src, dst, sem, at):
        return pltpu.make_async_copy(src, dst, sem.at[at])

    load_sol = local(sol_ref, sol_v, load_sem, 0)
    load_sol.start()
    load_wb = local(wb_ref, wb_v, load_sem, 1)
    load_map = local(
        map_ref.at[:, pl.ds(pl.multiple_of(r * 512, 512), 512)], map_v, load_sem, 2)
    load_ranks = local(ranks_ref, ranks_s, load_sem, 3)
    load_right = local(
        right_ref.at[:, pl.ds(pl.multiple_of((r // 4) * 8, 8), 8), :], right_v, load_sem, 4)
    load_inv = local(
        inv_ref.at[pl.ds(2 * r, 2)], invg.at[r], load_sem, 5)

    barrier = pltpu.get_barrier_semaphore()
    for d in NEAR:
        pl.semaphore_signal(barrier, inc=1, device_id={"col": lax.rem(c + d, N)}, device_id_type=MESH)
    for d in FAR_FIRST:
        pl.semaphore_signal(barrier, inc=1, device_id={"row": lax.rem(r + d, N)}, device_id_type=MESH)

    def loop(count, body):
        def step(n, carry):
            body(n)
            return carry

        lax.fori_loop(0, count, step, 0)

    def all_seven(ref, sem):
        seven = ref.at[pl.ds(0, N - 1)]
        pltpu.make_async_copy(seven, seven, sem.at[0]).wait()

    def away(n):
        return 4 + (n + 1) // 2 * (1 - 2 * lax.rem(n, 2))

    load_wb.start()
    load_map.start()
    load_ranks.start()
    load_right.start()
    load_inv.start()
    def load_basis(j):
        return local(basis_ref.at[j], basis_v.at[j], basis_sem, j)

    loop(N, lambda j: load_basis(j).start())

    load_sol.wait()
    sol_f[...] = sol_v[...].astype(F32).reshape(512, 64)
    for jj in range(4):
        both = jnp.concatenate(
            [sol_f[pl.ds(2 * jj + h, 64, stride=8), :] for h in range(2)], axis=0)
        gath[jj, c] = both.T.astype(BF16)

    pl.semaphore_wait(barrier, len(NEAR) + len(FAR_FIRST))

    def chunk(jj, slot, to, lane):
        slot, to = lax.rem(c + slot + N, N), lax.rem(c + to + N, N)
        return remote(gath.at[jj, slot], gath.at[jj, slot], ring_send, ring_recv, (lane, jj), "col", to)

    def direct(jj):
        chunk(jj, 0, 2, 0).start()
        chunk(jj, 0, -2, 1).start()

    def next_to(jj):
        chunk(jj, 0, 1, 2).start()
        chunk(jj, 0, -1, 3).start()

    loop(4, direct)
    loop(4, next_to)

    def tile_rows(d, to):
        return remote(inv_ref.at[pl.ds(2 * to, 2)], invg.at[r], inv_send, inv_recv, 0, "row", to)

    loop(N - 1, lambda n: tile_rows(away(n), lax.rem(r + away(n), N)).start())

    def relay(jj):
        way = 1 - 2 * lax.rem(jj, 2)
        for side in (1, -1):
            chunk(jj, -2 * side, 2 * side, (1 - side) // 2).wait_recv()

            @pl.when(way == side)
            def _(side=side):
                chunk(jj, -2 * side, 2 * side, 6).start()

            chunk(jj, -2 * side, side, 4 + (1 - side) // 2).start()

    load_wb.wait()
    row_i, col_i = iota((256, 256), 0), iota((256, 256), 1)
    perm = jnp.where(
        ((row_i >> 4) == (col_i & 15)) & ((row_i & 15) == (col_i >> 4)), 1.0, 0.0).astype(BF16)

    def regroup(step):
        jj, kb = step // 4, lax.rem(step, 4)
        k0 = pl.multiple_of(kb * 16, 16)
        x = jnp.concatenate(
            [wb_v[2 * jj + h, pl.ds(k0, 16)].reshape(256, 64) for h in range(2)], axis=1)
        y = dot(perm, x).astype(BF16).reshape(16, 16, 128)
        w0[:, pl.ds(pl.multiple_of(jj * 64 + kb * 16, 16), 16), :] = y

    loop(16, regroup)
    loop(4, relay)

    low = iota((1, 128), 1) < 64

    def coeffs(jj, first):
        pairs = [lax.rem(first + k, 4) for k in range(2)]
        g = jnp.concatenate([gath[jj, pl.ds(2 * p, 2)].reshape(128, 128) for p in pairs], axis=0)
        both = []
        for h in range(2):
            cols = [pl.ds(pl.multiple_of(p * 128, 128), 128) for p in pairs]
            both.append(dot(jnp.concatenate([basis_v[2 * jj + h, :, at] for at in cols], axis=1), g))
        return jnp.where(low, both[0], both[1])

    near = lax.rem((c + 7) // 2, 4)

    def near_half(jj):
        chunk(jj, 0, 1, 2).wait_recv()
        chunk(jj, 0, 1, 3).wait_recv()
        load_basis(2 * jj).wait()
        load_basis(2 * jj + 1).wait()
        half[jj] = coeffs(jj, near)

    loop(4, near_half)

    def turn(i):
        wt[i] = w0[i].T

    loop(16, turn)
    load_ranks.wait()
    k_of = iota((64, 128), 0)

    def far_half(jj):
        for lane in (4, 5, 6):
            chunk(jj, 0, 1, lane).wait_recv()
        total = half[jj] + coeffs(jj, lax.rem(near + 2, 4))
        for i in range(16):
            limit = jnp.where(low, ranks_s[2 * jj, i], ranks_s[2 * jj + 1, i])
            cut = jnp.where(k_of < limit, total[i * 64:(i + 1) * 64], 0.0)
            cm[i, pl.ds(pl.multiple_of(jj * 64, 64), 64), :] = cut.astype(BF16)

    loop(4, far_half)

    def update(to):
        sums = []
        for h in range(2):
            u = dot(wt[2 * to + h], cm[2 * to + h])
            sums.append(jnp.where(low, u[0:64], u[64:128]))
        return jnp.where(low, sums[0], sums[1]) + swap(jnp.where(low, sums[1], sums[0]))

    def p2(d, to):
        return remote(msg.at[d], part.at[d], p2_send, p2_recv, 0, "row", to)

    def send_update(n):
        d = away(n)
        to = lax.rem(r + d, N)
        msg[d] = update(to).astype(BF16)
        p2(d, to).start()

    loop(N - 1, send_update)
    own_update = update(r)

    load_map.wait()
    w = map_v[...]
    cc = (w >> 3) & 7
    code = (((w >> 9) & 1) << 9) + ((w >> 10) << 6) + (((w >> 6) & 7) << 3) + (w & 7) + 1
    mine = cc == c
    mine_f = jnp.where(mine, 1.0, 0.0)
    mine8 = jnp.where(iota((8, 512), 0) == 0, mine_f[0:1], mine_f[1:2]).astype(BF16)
    ta, tb = iota((512, 512), 0), iota((512, 512), 1)
    same = (ta >> 6) == (tb >> 6)
    before = dot(mine8, jnp.where(same & (ta < tb), 1.0, 0.0).astype(BF16))
    total = dot(mine8, jnp.where(same, 1.0, 0.0).astype(BF16))
    place = (before[0:1].astype(I32), (before[1:2] + total[0:1]).astype(I32))
    code_f = jnp.where(mine, code, 0).astype(F32)
    slots = []
    for g in range(4):
        at = slice(g * 128, (g + 1) * 128)
        ra, la = iota((64, 128), 0), iota((64, 128), 1)
        ours = (ra >> 5) == (la >> 6)
        acc = jnp.zeros((64, 128), F32)
        for ch in range(2):
            take = ours & ((ra & 31) == place[ch][:, at])
            acc = acc + jnp.where(take, code_f[ch:ch + 1, at], 0.0)
        slots.append(jnp.sum(acc, axis=1, keepdims=True))
    slot = jnp.concatenate(slots, axis=0).astype(I32)
    src = iota((256, 512), 1) + 1
    for h in range(2):
        selm[h * 256:(h + 1) * 256, :] = jnp.where(src + h * 512 == slot, 1.0, 0.0).astype(BF16)
    ra, la = iota((64, 512), 0), iota((64, 512), 1)
    selm[512:576, :] = jnp.where(
        la == ((ra >> 3) << 6) + r * 8 + (ra & 7), 1.0, 0.0).astype(BF16)

    load_right.wait()
    right_f[...] = right_v[...].reshape(512, 64)
    base = 2 * lax.rem(r, 4)
    right_t = jnp.concatenate(
        [right_f[pl.ds(base + h, 64, stride=8), :] for h in range(2)], axis=0).T

    acc = right_t - own_update
    all_seven(part, p2_recv)
    for d in range(1, N):
        acc = acc - part[d].astype(F32)
    red[...] = acc.astype(BF16)
    redg[c] = acc.astype(BF16)

    def p3(d, to):
        return remote(red, redg.at[c], p3_send, p3_recv, 0, "col", to)

    loop(N - 1, lambda n: p3(away(n), lax.rem(c + away(n), N)).start())
    load_inv.wait()
    all_seven(invg, inv_recv)
    for h in range(2):
        invl[h * 64:(h + 1) * 64, :] = invg[:, h].astype(F32).reshape(64, 512).astype(BF16)

    x = map_v[:, pl.ds(pl.multiple_of((c // 2) * 128, 128), 128)]
    x_swapped = swap(x)
    odd = lax.rem(c, 2) == 1
    own = jnp.where(
        low, jnp.where(odd, x_swapped[0:1], x[0:1]), jnp.where(odd, x[1:2], x_swapped[1:2]))
    class_l = ((own >> 3) & 7).astype(F32)
    qa, qb = iota((128, 128), 0), iota((128, 128), 1)
    class_s = jnp.sum(jnp.where(qa == qb, class_l, 0.0), axis=1, keepdims=True)
    rank_s = jnp.sum(jnp.where((class_s == class_l) & (qb < qa), 1.0, 0.0), axis=1, keepdims=True)
    rank_i = rank_s.astype(I32)
    found = class_s.astype(I32) * 16 + (rank_i & 15)
    for h in range(2):
        s5[h] = jnp.where((qb == found) & ((rank_i >> 4) == h), 1.0, 0.0).astype(BF16)

    all_seven(redg, p3_recv)

    s = dot(invl[...], redg[...].reshape(512, 128))
    solved = jnp.where(low, s[0:64], s[64:128]).astype(BF16)
    solg[r] = solved

    def p4(d, to):
        return remote(solg.at[r], solg.at[r], p4_send, p4_recv, 0, "row", to)

    loop(N - 1, lambda n: p4(away(n), lax.rem(r + away(n), N)).start())
    all_seven(solg, p4_recv)

    picked = dot(selm[...], solg[...].reshape(512, 128))
    rows = jnp.where(low, picked[0:256], picked[256:512])
    rows = (rows + swap(rows)).reshape(8, 32, 128)
    pk[...] = jnp.where(low, rows[:, 0:16], rows[:, 16:32]).astype(BF16)
    chg[c] = pk[c]

    def p5(d, to):
        return remote(pk.at[to], chg.at[c], p5_send, p5_recv, 0, "col", to)

    loop(N - 1, lambda n: p5(away(n), lax.rem(c + away(n), N)).start())

    own_rows = picked[512:576]
    out_sol[:, 0] = own_rows[:, 0:64].reshape(8, 8, 64).astype(BF16)
    out_sol[:, 1] = swap(own_rows)[:, 0:64].reshape(8, 8, 64).astype(BF16)

    def sent(n):
        chunk(n // 7, 0, 1, lax.rem(n, 7)).wait_send()

    loop(28, sent)
    all_seven(invg, inv_send)
    all_seven(msg, p2_send)
    all_seven(redg, p3_send)
    all_seven(solg, p4_send)

    all_seven(chg, p5_recv)
    got = chg[...].reshape(128, 128)
    child = jnp.where(low, dot(s5[0], got), dot(s5[1], got))
    child = child + swap(child)
    out_child[...] = child.T[0:64].astype(BF16)
    all_seven(pk, p5_send)


def on_device(right_side, rest_solution, rest_basis, window_basis, ranks, inverses, child_map):
    any_spec = pl.BlockSpec(memory_space=pl.ANY)
    vmem_spec = pl.BlockSpec(memory_space=pltpu.VMEM)
    dma = pltpu.SemaphoreType.DMA
    sol, child = pl.pallas_call(
        kernel,
        out_shape=(
            pltpu.VMEM((8, 2, 8, 64), BF16),
            pltpu.VMEM((64, 128), BF16),
        ),
        in_specs=[any_spec] * 7,
        out_specs=(vmem_spec, vmem_spec),
        scratch_shapes=[
            pltpu.VMEM((64, 8, 64), BF16),
            pltpu.VMEM((512, 64), F32),
            pltpu.VMEM((64, 8, 64), F32),
            pltpu.VMEM((512, 64), F32),
            pltpu.VMEM((8, 1024, 512), BF16),
            pltpu.VMEM((8, 64, 16, 64), BF16),
            pltpu.VMEM((2, 512), I32),
            pltpu.SMEM((8, 16), I32),
            pltpu.VMEM((4, 8, 64, 128), BF16),
            pltpu.VMEM((4, 1024, 128), F32),
            pltpu.VMEM((16, 256, 128), BF16),
            pltpu.VMEM((16, 128, 256), BF16),
            pltpu.VMEM((16, 256, 128), BF16),
            pltpu.VMEM((8, 64, 128), BF16),
            pltpu.VMEM((8, 64, 128), BF16),
            pltpu.VMEM((64, 128), BF16),
            pltpu.VMEM((8, 64, 128), BF16),
            pltpu.VMEM((8, 2, 8, 512), BF16),
            pltpu.VMEM((128, 512), BF16),
            pltpu.VMEM((8, 64, 128), BF16),
            pltpu.VMEM((576, 512), BF16),
            pltpu.VMEM((2, 128, 128), BF16),
            pltpu.VMEM((8, 16, 128), BF16),
            pltpu.VMEM((8, 16, 128), BF16),
            dma((6,)), dma((8,)), dma((7, 4)), dma((7, 4)),
            dma((1,)), dma((1,)),
            dma((1,)), dma((1,)), dma((1,)), dma((1,)),
            dma((1,)), dma((1,)), dma((1,)), dma((1,)),
        ],
        compiler_params=pltpu.CompilerParams(
            collective_id=0, has_side_effects=True, vmem_limit_bytes=56 * 1024 * 1024
        ),
        cost_estimate=pl.CostEstimate(flops=700_000_000, bytes_accessed=12_000_000, transcendentals=0),
    )(right_side, rest_solution, rest_basis, window_basis, ranks, inverses, child_map)
    solution_rows = sol.reshape(16, 8, 64).transpose(2, 0, 1)
    return solution_rows, child.reshape(64, 2, 64)


def solution(mesh):
    in_specs = (
        P("shot", None, "col"),
        P("shot", "row", "col"),
        P("row", None, None),
        P("row", None, None, "col"),
        P("row", None),
        P(None, ("row", "col"), None),
        P(),
    )
    out_specs = (P("shot", None, ("row", "col")), P("shot", None, ("row", "col")))
    return jax.shard_map(
        on_device, mesh=mesh, in_specs=in_specs, out_specs=out_specs, check_vma=False
    )
```

```python
import jax
import jax.numpy as jnp
from jax import lax
from jax.experimental import pallas as pl
from jax.experimental.pallas import tpu as pltpu
from jax.sharding import PartitionSpec as P

MESH = pl.DeviceIdType.MESH
F32 = jnp.float32
BF16 = jnp.bfloat16
I32 = jnp.int32
N = 8
NEAR = (2, 6, 1, 7)
FAR_FIRST = (4, 3, 5, 2, 6, 1, 7)


def iota(shape, axis):
    return lax.broadcasted_iota(I32, shape, axis)


def dot(a, b):
    return jnp.dot(a, b, preferred_element_type=F32)


def swap(x):
    return pltpu.roll(x, 64, 1)


def kernel(
    right_ref, sol_ref, basis_ref, wb_ref, ranks_ref, inv_ref, map_ref,
    out_sol, out_child,
    sol_v, sol_f, right_v, right_f, basis_v, wb_v, map_v, ranks_s,
    gath, half, w0, wt, cm, msg, part, red, redg, invg, invl, solg, selm, s5, pk, chg,
    load_sem, basis_sem, ring_send, ring_recv, inv_send, inv_recv,
    p2_send, p2_recv, p3_send, p3_recv, p4_send, p4_recv, p5_send, p5_recv,
):
    r = lax.axis_index("row")
    c = lax.axis_index("col")

    def remote(src, dst, send, recv, at, axis, to):
        return pltpu.make_async_remote_copy(
            src_ref=src, dst_ref=dst, send_sem=send.at[at], recv_sem=recv.at[at],
            device_id={axis: to}, device_id_type=MESH,
        )

    def local(src, dst, sem, at):
        return pltpu.make_async_copy(src, dst, sem.at[at])

    load_sol = local(sol_ref, sol_v, load_sem, 0)
    load_sol.start()
    load_wb = local(wb_ref, wb_v, load_sem, 1)
    load_map = local(
        map_ref.at[:, pl.ds(pl.multiple_of(r * 512, 512), 512)], map_v, load_sem, 2)
    load_ranks = local(ranks_ref, ranks_s, load_sem, 3)
    load_right = local(
        right_ref.at[:, pl.ds(pl.multiple_of((r // 4) * 8, 8), 8), :], right_v, load_sem, 4)
    load_inv = local(
        inv_ref.at[pl.ds(2 * r, 2)], invg.at[r], load_sem, 5)

    barrier = pltpu.get_barrier_semaphore()
    for d in NEAR:
        pl.semaphore_signal(barrier, inc=1, device_id={"col": lax.rem(c + d, N)}, device_id_type=MESH)
    for d in FAR_FIRST:
        pl.semaphore_signal(barrier, inc=1, device_id={"row": lax.rem(r + d, N)}, device_id_type=MESH)

    def loop(count, body):
        def step(n, carry):
            body(n)
            return carry

        lax.fori_loop(0, count, step, 0)

    def all_seven(ref, sem):
        seven = ref.at[pl.ds(0, N - 1)]
        pltpu.make_async_copy(seven, seven, sem.at[0]).wait()

    def away(n):
        return 4 + (n + 1) // 2 * (1 - 2 * lax.rem(n, 2))

    load_wb.start()
    load_map.start()
    load_ranks.start()
    load_right.start()
    load_inv.start()
    def load_basis(j):
        return local(basis_ref.at[j], basis_v.at[j], basis_sem, j)

    loop(N, lambda j: load_basis(j).start())

    load_sol.wait()
    sol_f[...] = sol_v[...].astype(F32).reshape(512, 64)
    for jj in range(4):
        both = jnp.concatenate(
            [sol_f[pl.ds(2 * jj + h, 64, stride=8), :] for h in range(2)], axis=0)
        gath[jj, c] = both.T.astype(BF16)

    pl.semaphore_wait(barrier, len(NEAR) + len(FAR_FIRST))

    def chunk(jj, slot, to, lane):
        slot, to = lax.rem(c + slot + N, N), lax.rem(c + to + N, N)
        return remote(gath.at[jj, slot], gath.at[jj, slot], ring_send, ring_recv, (lane, jj), "col", to)

    def direct(jj):
        chunk(jj, 0, 2, 0).start()
        chunk(jj, 0, -2, 1).start()

    def next_to(jj):
        chunk(jj, 0, 1, 2).start()
        chunk(jj, 0, -1, 3).start()

    loop(4, direct)
    loop(4, next_to)

    def tile_rows(d, to):
        return remote(inv_ref.at[pl.ds(2 * to, 2)], invg.at[r], inv_send, inv_recv, 0, "row", to)

    loop(N - 1, lambda n: tile_rows(away(n), lax.rem(r + away(n), N)).start())

    def relay(jj):
        way = 1 - 2 * lax.rem(jj, 2)
        for side in (1, -1):
            chunk(jj, -2 * side, 2 * side, (1 - side) // 2).wait_recv()

            @pl.when(way == side)
            def _(side=side):
                chunk(jj, -2 * side, 2 * side, 6).start()

            chunk(jj, -2 * side, side, 4 + (1 - side) // 2).start()

    load_wb.wait()
    row_i, col_i = iota((256, 256), 0), iota((256, 256), 1)
    perm = jnp.where(
        ((row_i >> 4) == (col_i & 15)) & ((row_i & 15) == (col_i >> 4)), 1.0, 0.0).astype(BF16)

    def regroup(step):
        jj, kb = step // 4, lax.rem(step, 4)
        k0 = pl.multiple_of(kb * 16, 16)
        x = jnp.concatenate(
            [wb_v[2 * jj + h, pl.ds(k0, 16)].reshape(256, 64) for h in range(2)], axis=1)
        y = dot(perm, x).astype(BF16).reshape(16, 16, 128)
        w0[:, pl.ds(pl.multiple_of(jj * 64 + kb * 16, 16), 16), :] = y

    def regroups(n):
        for k in range(4):
            regroup(4 * n + k)

    loop(4, regroups)

    def turn(i):
        wt[i] = w0[i].T

    def turns(n):
        for k in range(4):
            turn(4 * n + k)

    loop(4, turns)
    loop(4, relay)

    low = iota((1, 128), 1) < 64

    def coeffs(jj, first):
        pairs = [lax.rem(first + k, 4) for k in range(2)]
        g = jnp.concatenate([gath[jj, pl.ds(2 * p, 2)].reshape(128, 128) for p in pairs], axis=0)
        both = []
        for h in range(2):
            cols = [pl.ds(pl.multiple_of(p * 128, 128), 128) for p in pairs]
            both.append(dot(jnp.concatenate([basis_v[2 * jj + h, :, at] for at in cols], axis=1), g))
        return jnp.where(low, both[0], both[1])

    near = lax.rem((c + 7) // 2, 4)

    def near_half(jj):
        chunk(jj, 0, 1, 2).wait_recv()
        chunk(jj, 0, 1, 3).wait_recv()
        load_basis(2 * jj).wait()
        load_basis(2 * jj + 1).wait()
        half[jj] = coeffs(jj, near)

    loop(4, near_half)

    load_ranks.wait()
    k_of = iota((64, 128), 0)

    def far_half(jj):
        for lane in (4, 5, 6):
            chunk(jj, 0, 1, lane).wait_recv()
        total = half[jj] + coeffs(jj, lax.rem(near + 2, 4))
        for i in range(16):
            limit = jnp.where(low, ranks_s[2 * jj, i], ranks_s[2 * jj + 1, i])
            cut = jnp.where(k_of < limit, total[i * 64:(i + 1) * 64], 0.0)
            cm[i, pl.ds(pl.multiple_of(jj * 64, 64), 64), :] = cut.astype(BF16)

    loop(4, far_half)

    def update(to):
        sums = []
        for h in range(2):
            u = dot(wt[2 * to + h], cm[2 * to + h])
            sums.append(jnp.where(low, u[0:64], u[64:128]))
        return jnp.where(low, sums[0], sums[1]) + swap(jnp.where(low, sums[1], sums[0]))

    def p2(d, to):
        return remote(msg.at[d], part.at[d], p2_send, p2_recv, 0, "row", to)

    def send_update(n):
        d = away(n)
        to = lax.rem(r + d, N)
        msg[d] = update(to).astype(BF16)
        p2(d, to).start()

    loop(N - 1, send_update)
    own_update = update(r)

    load_map.wait()
    w = map_v[...]
    cc = (w >> 3) & 7
    code = (((w >> 9) & 1) << 9) + ((w >> 10) << 6) + (((w >> 6) & 7) << 3) + (w & 7) + 1
    mine = cc == c
    mine_f = jnp.where(mine, 1.0, 0.0)
    mine8 = jnp.where(iota((8, 512), 0) == 0, mine_f[0:1], mine_f[1:2]).astype(BF16)
    ta, tb = iota((512, 512), 0), iota((512, 512), 1)
    same = (ta >> 6) == (tb >> 6)
    before = dot(mine8, jnp.where(same & (ta < tb), 1.0, 0.0).astype(BF16))
    total = dot(mine8, jnp.where(same, 1.0, 0.0).astype(BF16))
    place = (before[0:1].astype(I32), (before[1:2] + total[0:1]).astype(I32))
    code_f = jnp.where(mine, code, 0).astype(F32)
    slots = []
    for g in range(4):
        at = slice(g * 128, (g + 1) * 128)
        ra, la = iota((64, 128), 0), iota((64, 128), 1)
        ours = (ra >> 5) == (la >> 6)
        acc = jnp.zeros((64, 128), F32)
        for ch in range(2):
            take = ours & ((ra & 31) == place[ch][:, at])
            acc = acc + jnp.where(take, code_f[ch:ch + 1, at], 0.0)
        slots.append(jnp.sum(acc, axis=1, keepdims=True))
    slot = jnp.concatenate(slots, axis=0).astype(I32)
    src = iota((256, 512), 1) + 1
    for h in range(2):
        selm[h * 256:(h + 1) * 256, :] = jnp.where(src + h * 512 == slot, 1.0, 0.0).astype(BF16)
    ra, la = iota((64, 512), 0), iota((64, 512), 1)
    selm[512:576, :] = jnp.where(
        la == ((ra >> 3) << 6) + r * 8 + (ra & 7), 1.0, 0.0).astype(BF16)

    load_right.wait()
    right_f[...] = right_v[...].reshape(512, 64)
    base = 2 * lax.rem(r, 4)
    right_t = jnp.concatenate(
        [right_f[pl.ds(base + h, 64, stride=8), :] for h in range(2)], axis=0).T

    acc = right_t - own_update
    all_seven(part, p2_recv)
    for d in range(1, N):
        acc = acc - part[d].astype(F32)
    red[...] = acc.astype(BF16)
    redg[c] = acc.astype(BF16)

    def p3(d, to):
        return remote(red, redg.at[c], p3_send, p3_recv, 0, "col", to)

    loop(N - 1, lambda n: p3(away(n), lax.rem(c + away(n), N)).start())
    load_inv.wait()
    all_seven(invg, inv_recv)
    for h in range(2):
        invl[h * 64:(h + 1) * 64, :] = invg[:, h].astype(F32).reshape(64, 512).astype(BF16)

    x = map_v[:, pl.ds(pl.multiple_of((c // 2) * 128, 128), 128)]
    x_swapped = swap(x)
    odd = lax.rem(c, 2) == 1
    own = jnp.where(
        low, jnp.where(odd, x_swapped[0:1], x[0:1]), jnp.where(odd, x[1:2], x_swapped[1:2]))
    class_l = ((own >> 3) & 7).astype(F32)
    qa, qb = iota((128, 128), 0), iota((128, 128), 1)
    class_s = jnp.sum(jnp.where(qa == qb, class_l, 0.0), axis=1, keepdims=True)
    rank_s = jnp.sum(jnp.where((class_s == class_l) & (qb < qa), 1.0, 0.0), axis=1, keepdims=True)
    rank_i = rank_s.astype(I32)
    found = class_s.astype(I32) * 16 + (rank_i & 15)
    for h in range(2):
        s5[h] = jnp.where((qb == found) & ((rank_i >> 4) == h), 1.0, 0.0).astype(BF16)

    all_seven(redg, p3_recv)

    s = dot(invl[...], redg[...].reshape(512, 128))
    solved = jnp.where(low, s[0:64], s[64:128]).astype(BF16)
    solg[r] = solved

    def p4(d, to):
        return remote(solg.at[r], solg.at[r], p4_send, p4_recv, 0, "row", to)

    loop(N - 1, lambda n: p4(away(n), lax.rem(r + away(n), N)).start())
    all_seven(solg, p4_recv)

    picked = dot(selm[...], solg[...].reshape(512, 128))
    rows = jnp.where(low, picked[0:256], picked[256:512])
    rows = (rows + swap(rows)).reshape(8, 32, 128)
    pk[...] = jnp.where(low, rows[:, 0:16], rows[:, 16:32]).astype(BF16)
    chg[c] = pk[c]

    def p5(d, to):
        return remote(pk.at[to], chg.at[c], p5_send, p5_recv, 0, "col", to)

    loop(N - 1, lambda n: p5(away(n), lax.rem(c + away(n), N)).start())

    own_rows = picked[512:576]
    out_sol[:, 0] = own_rows[:, 0:64].reshape(8, 8, 64).astype(BF16)
    out_sol[:, 1] = swap(own_rows)[:, 0:64].reshape(8, 8, 64).astype(BF16)

    def sent(n):
        chunk(n // 7, 0, 1, lax.rem(n, 7)).wait_send()

    loop(28, sent)
    all_seven(invg, inv_send)
    all_seven(msg, p2_send)
    all_seven(redg, p3_send)
    all_seven(solg, p4_send)

    all_seven(chg, p5_recv)
    got = chg[...].reshape(128, 128)
    child = jnp.where(low, dot(s5[0], got), dot(s5[1], got))
    child = child + swap(child)
    out_child[...] = child.T[0:64].astype(BF16)
    all_seven(pk, p5_send)


def on_device(right_side, rest_solution, rest_basis, window_basis, ranks, inverses, child_map):
    any_spec = pl.BlockSpec(memory_space=pl.ANY)
    vmem_spec = pl.BlockSpec(memory_space=pltpu.VMEM)
    dma = pltpu.SemaphoreType.DMA
    sol, child = pl.pallas_call(
        kernel,
        out_shape=(
            pltpu.VMEM((8, 2, 8, 64), BF16),
            pltpu.VMEM((64, 128), BF16),
        ),
        in_specs=[any_spec] * 7,
        out_specs=(vmem_spec, vmem_spec),
        scratch_shapes=[
            pltpu.VMEM((64, 8, 64), BF16),
            pltpu.VMEM((512, 64), F32),
            pltpu.VMEM((64, 8, 64), F32),
            pltpu.VMEM((512, 64), F32),
            pltpu.VMEM((8, 1024, 512), BF16),
            pltpu.VMEM((8, 64, 16, 64), BF16),
            pltpu.VMEM((2, 512), I32),
            pltpu.SMEM((8, 16), I32),
            pltpu.VMEM((4, 8, 64, 128), BF16),
            pltpu.VMEM((4, 1024, 128), F32),
            pltpu.VMEM((16, 256, 128), BF16),
            pltpu.VMEM((16, 128, 256), BF16),
            pltpu.VMEM((16, 256, 128), BF16),
            pltpu.VMEM((8, 64, 128), BF16),
            pltpu.VMEM((8, 64, 128), BF16),
            pltpu.VMEM((64, 128), BF16),
            pltpu.VMEM((8, 64, 128), BF16),
            pltpu.VMEM((8, 2, 8, 512), BF16),
            pltpu.VMEM((128, 512), BF16),
            pltpu.VMEM((8, 64, 128), BF16),
            pltpu.VMEM((576, 512), BF16),
            pltpu.VMEM((2, 128, 128), BF16),
            pltpu.VMEM((8, 16, 128), BF16),
            pltpu.VMEM((8, 16, 128), BF16),
            dma((6,)), dma((8,)), dma((7, 4)), dma((7, 4)),
            dma((1,)), dma((1,)),
            dma((1,)), dma((1,)), dma((1,)), dma((1,)),
            dma((1,)), dma((1,)), dma((1,)), dma((1,)),
        ],
        compiler_params=pltpu.CompilerParams(
            collective_id=0, has_side_effects=True, vmem_limit_bytes=56 * 1024 * 1024
        ),
        cost_estimate=pl.CostEstimate(flops=700_000_000, bytes_accessed=12_000_000, transcendentals=0),
    )(right_side, rest_solution, rest_basis, window_basis, ranks, inverses, child_map)
    solution_rows = sol.reshape(16, 8, 64).transpose(2, 0, 1)
    return solution_rows, child.reshape(64, 2, 64)


def solution(mesh):
    in_specs = (
        P("shot", None, "col"),
        P("shot", "row", "col"),
        P("row", None, None),
        P("row", None, None, "col"),
        P("row", None),
        P(None, ("row", "col"), None),
        P(),
    )
    out_specs = (P("shot", None, ("row", "col")), P("shot", None, ("row", "col")))
    return jax.shard_map(
        on_device, mesh=mesh, in_specs=in_specs, out_specs=out_specs, check_vma=False
    )
```

```python
import jax
import jax.numpy as jnp
from jax import lax
from jax.experimental import pallas as pl
from jax.experimental.pallas import tpu as pltpu
from jax.sharding import PartitionSpec as P

MESH = pl.DeviceIdType.MESH
F32 = jnp.float32
BF16 = jnp.bfloat16
I32 = jnp.int32
N = 8
NEAR = (2, 6, 1, 7)
ROW_ORDER = (4, 5, 2, 3, 6, 7, 1)
FAR_FIRST = (4, 3, 5, 2, 6, 1, 7)


def iota(shape, axis):
    return lax.broadcasted_iota(I32, shape, axis)


def dot(a, b):
    return jnp.dot(a, b, preferred_element_type=F32)


def swap(x):
    return pltpu.roll(x, 64, 1)


def kernel(
    right_ref, sol_ref, basis_ref, wb_ref, ranks_ref, inv_ref, map_ref,
    out_sol, out_child,
    sol_v, sol_f, right_v, right_f, basis_v, wb_v, map_v, ranks_s,
    gath, half, w0, wt, cm, msg, part, red, redg, invg, invl, solg, selm, s5, pk, chg,
    load_sem, basis_sem, ring_send, ring_recv, inv_send, inv_recv,
    p2_send, p2_recv, p3_send, p3_recv, p4_send, p4_recv, p5_send, p5_recv,
):
    r = lax.axis_index("row")
    c = lax.axis_index("col")

    def remote(src, dst, send, recv, at, axis, to):
        return pltpu.make_async_remote_copy(
            src_ref=src, dst_ref=dst, send_sem=send.at[at], recv_sem=recv.at[at],
            device_id={axis: to}, device_id_type=MESH,
        )

    def local(src, dst, sem, at):
        return pltpu.make_async_copy(src, dst, sem.at[at])

    load_sol = local(sol_ref, sol_v, load_sem, 0)
    load_sol.start()
    load_wb = local(wb_ref, wb_v, load_sem, 1)
    load_map = local(
        map_ref.at[:, pl.ds(pl.multiple_of(r * 512, 512), 512)], map_v, load_sem, 2)
    load_ranks = local(ranks_ref, ranks_s, load_sem, 3)
    load_right = local(
        right_ref.at[:, pl.ds(pl.multiple_of((r // 4) * 8, 8), 8), :], right_v, load_sem, 4)
    load_inv = local(
        inv_ref.at[pl.ds(2 * r, 2)], invg.at[r], load_sem, 5)

    barrier = pltpu.get_barrier_semaphore()
    for d in NEAR:
        pl.semaphore_signal(barrier, inc=1, device_id={"col": lax.rem(c + d, N)}, device_id_type=MESH)
    for d in FAR_FIRST:
        pl.semaphore_signal(barrier, inc=1, device_id={"row": lax.rem(r + d, N)}, device_id_type=MESH)

    def loop(count, body):
        def step(n, carry):
            body(n)
            return carry

        lax.fori_loop(0, count, step, 0)

    def all_seven(ref, sem):
        seven = ref.at[pl.ds(0, N - 1)]
        pltpu.make_async_copy(seven, seven, sem.at[0]).wait()

    def row_at(k):
        return lax.rem(r // 2 + k // 2, 4) * 2 + lax.rem(r + k % 2, 2)

    def arrived(ref, sem, far):
        some = ref.at[pl.ds(0, 2 if far else 5)]
        pltpu.make_async_copy(some, some, sem.at[far]).wait()

    def away(n):
        return 4 + (n + 1) // 2 * (1 - 2 * lax.rem(n, 2))

    load_wb.start()
    load_map.start()
    load_ranks.start()
    load_right.start()
    load_inv.start()
    def load_basis(j):
        return local(basis_ref.at[j], basis_v.at[j], basis_sem, j)

    loop(N, lambda j: load_basis(j).start())

    load_sol.wait()
    sol_f[...] = sol_v[...].astype(F32).reshape(512, 64)
    for jj in range(4):
        both = jnp.concatenate(
            [sol_f[pl.ds(2 * jj + h, 64, stride=8), :] for h in range(2)], axis=0)
        gath[jj, c] = both.T.astype(BF16)

    pl.semaphore_wait(barrier, len(NEAR) + len(FAR_FIRST))

    def chunk(jj, slot, to, lane):
        slot, to = lax.rem(c + slot + N, N), lax.rem(c + to + N, N)
        return remote(gath.at[jj, slot], gath.at[jj, slot], ring_send, ring_recv, (lane, jj), "col", to)

    def direct(jj):
        chunk(jj, 0, 2, 0).start()
        chunk(jj, 0, -2, 1).start()

    def next_to(jj):
        chunk(jj, 0, 1, 2).start()
        chunk(jj, 0, -1, 3).start()

    loop(4, direct)
    loop(4, next_to)

    def tile_rows(d, to):
        return remote(inv_ref.at[pl.ds(2 * to, 2)], invg.at[r], inv_send, inv_recv, 0, "row", to)

    loop(N - 1, lambda n: tile_rows(away(n), lax.rem(r + away(n), N)).start())

    def relay(jj):
        way = 1 - 2 * lax.rem(jj, 2)
        for side in (1, -1):
            chunk(jj, -2 * side, 2 * side, (1 - side) // 2).wait_recv()

            @pl.when(way == side)
            def _(side=side):
                chunk(jj, -2 * side, 2 * side, 6).start()

            chunk(jj, -2 * side, side, 4 + (1 - side) // 2).start()

    load_wb.wait()
    row_i, col_i = iota((256, 256), 0), iota((256, 256), 1)
    perm = jnp.where(
        ((row_i >> 4) == (col_i & 15)) & ((row_i & 15) == (col_i >> 4)), 1.0, 0.0).astype(BF16)

    def regroup(step):
        jj, kb = step // 4, lax.rem(step, 4)
        k0 = pl.multiple_of(kb * 16, 16)
        x = jnp.concatenate(
            [wb_v[2 * jj + h, pl.ds(k0, 16)].reshape(256, 64) for h in range(2)], axis=1)
        y = dot(perm, x).astype(BF16).reshape(16, 16, 128)
        w0[:, pl.ds(pl.multiple_of(jj * 64 + kb * 16, 16), 16), :] = y

    def regroups(n):
        for k in range(4):
            regroup(4 * n + k)

    loop(4, regroups)

    def turn(i):
        wt[i] = w0[i].T

    def turns(n):
        for k in range(4):
            turn(4 * n + k)

    loop(4, turns)
    loop(4, relay)

    low = iota((1, 128), 1) < 64

    def coeffs(jj, first):
        pairs = [lax.rem(first + k, 4) for k in range(2)]
        g = jnp.concatenate([gath[jj, pl.ds(2 * p, 2)].reshape(128, 128) for p in pairs], axis=0)
        both = []
        for h in range(2):
            cols = [pl.ds(pl.multiple_of(p * 128, 128), 128) for p in pairs]
            both.append(dot(jnp.concatenate([basis_v[2 * jj + h, :, at] for at in cols], axis=1), g))
        return jnp.where(low, both[0], both[1])

    near = lax.rem((c + 7) // 2, 4)

    def near_half(jj):
        chunk(jj, 0, 1, 2).wait_recv()
        chunk(jj, 0, 1, 3).wait_recv()
        load_basis(2 * jj).wait()
        load_basis(2 * jj + 1).wait()
        half[jj] = coeffs(jj, near)

    loop(4, near_half)

    load_ranks.wait()
    k_of = iota((64, 128), 0)

    def far_half(jj):
        for lane in (4, 5, 6):
            chunk(jj, 0, 1, lane).wait_recv()
        total = half[jj] + coeffs(jj, lax.rem(near + 2, 4))
        for i in range(16):
            limit = jnp.where(low, ranks_s[2 * jj, i], ranks_s[2 * jj + 1, i])
            cut = jnp.where(k_of < limit, total[i * 64:(i + 1) * 64], 0.0)
            cm[i, pl.ds(pl.multiple_of(jj * 64, 64), 64), :] = cut.astype(BF16)

    loop(4, far_half)

    def update(to):
        sums = []
        for h in range(2):
            u = dot(wt[2 * to + h], cm[2 * to + h])
            sums.append(jnp.where(low, u[0:64], u[64:128]))
        return jnp.where(low, sums[0], sums[1]) + swap(jnp.where(low, sums[1], sums[0]))

    def p2(d, to):
        return remote(msg.at[d], part.at[d], p2_send, p2_recv, int(d // 2 == 2), "row", to)

    for k in ROW_ORDER:
        msg[k] = update(row_at(k)).astype(BF16)
        p2(k, row_at(k)).start()
    own_update = update(r)

    load_map.wait()
    w = map_v[...]
    cc = (w >> 3) & 7
    code = (((w >> 9) & 1) << 9) + ((w >> 10) << 6) + (((w >> 6) & 7) << 3) + (w & 7) + 1
    mine = cc == c
    mine_f = jnp.where(mine, 1.0, 0.0)
    mine8 = jnp.where(iota((8, 512), 0) == 0, mine_f[0:1], mine_f[1:2]).astype(BF16)
    ta, tb = iota((512, 512), 0), iota((512, 512), 1)
    same = (ta >> 6) == (tb >> 6)
    before = dot(mine8, jnp.where(same & (ta < tb), 1.0, 0.0).astype(BF16))
    total = dot(mine8, jnp.where(same, 1.0, 0.0).astype(BF16))
    place = (before[0:1].astype(I32), (before[1:2] + total[0:1]).astype(I32))
    code_f = jnp.where(mine, code, 0).astype(F32)
    slots = []
    for g in range(4):
        at = slice(g * 128, (g + 1) * 128)
        ra, la = iota((64, 128), 0), iota((64, 128), 1)
        ours = (ra >> 5) == (la >> 6)
        acc = jnp.zeros((64, 128), F32)
        for ch in range(2):
            take = ours & ((ra & 31) == place[ch][:, at])
            acc = acc + jnp.where(take, code_f[ch:ch + 1, at], 0.0)
        slots.append(jnp.sum(acc, axis=1, keepdims=True))
    slot = jnp.concatenate(slots, axis=0).astype(I32)
    src = iota((256, 512), 1) + 1
    for h in range(2):
        selm[h * 256:(h + 1) * 256, :] = jnp.where(src + h * 512 == slot, 1.0, 0.0).astype(BF16)
    ra, la = iota((64, 512), 0), iota((64, 512), 1)
    selm[512:576, :] = jnp.where(
        la == ((ra >> 3) << 6) + r * 8 + (ra & 7), 1.0, 0.0).astype(BF16)

    load_right.wait()
    right_f[...] = right_v[...].reshape(512, 64)
    base = 2 * lax.rem(r, 4)
    right_t = jnp.concatenate(
        [right_f[pl.ds(base + h, 64, stride=8), :] for h in range(2)], axis=0).T

    acc = right_t - own_update
    for far in (0, 1):
        arrived(part, p2_recv, far)
        for k in ROW_ORDER:
            if int(k // 2 == 2) == far:
                acc = acc - part[k].astype(F32)
    red[...] = acc.astype(BF16)
    redg[c] = acc.astype(BF16)

    def p3(d, to):
        return remote(red, redg.at[c], p3_send, p3_recv, 0, "col", to)

    loop(N - 1, lambda n: p3(away(n), lax.rem(c + away(n), N)).start())
    load_inv.wait()
    all_seven(invg, inv_recv)
    for h in range(2):
        invl[h * 64:(h + 1) * 64, :] = invg[:, h].astype(F32).reshape(64, 512).astype(BF16)

    x = map_v[:, pl.ds(pl.multiple_of((c // 2) * 128, 128), 128)]
    x_swapped = swap(x)
    odd = lax.rem(c, 2) == 1
    own = jnp.where(
        low, jnp.where(odd, x_swapped[0:1], x[0:1]), jnp.where(odd, x[1:2], x_swapped[1:2]))
    class_l = ((own >> 3) & 7).astype(F32)
    qa, qb = iota((128, 128), 0), iota((128, 128), 1)
    class_s = jnp.sum(jnp.where(qa == qb, class_l, 0.0), axis=1, keepdims=True)
    rank_s = jnp.sum(jnp.where((class_s == class_l) & (qb < qa), 1.0, 0.0), axis=1, keepdims=True)
    rank_i = rank_s.astype(I32)
    found = class_s.astype(I32) * 16 + (rank_i & 15)
    for h in range(2):
        s5[h] = jnp.where((qb == found) & ((rank_i >> 4) == h), 1.0, 0.0).astype(BF16)

    all_seven(redg, p3_recv)

    s = dot(invl[...], redg[...].reshape(512, 128))
    solved = jnp.where(low, s[0:64], s[64:128]).astype(BF16)
    solg[r] = solved

    def p4(d, to):
        return remote(solg.at[r], solg.at[r], p4_send, p4_recv, int(d // 2 == 2), "row", to)

    for k in ROW_ORDER:
        p4(k, row_at(k)).start()

    def picked_from(chips):
        at = [lax.rem(r // 2 + k, 4) for k in chips]
        table = jnp.concatenate([selm[:, pl.ds(pl.multiple_of(p * 128, 128), 128)] for p in at], axis=1)
        rows = jnp.concatenate([solg[pl.ds(2 * p, 2)].reshape(128, 128) for p in at], axis=0)
        return dot(table, rows)

    arrived(solg, p4_recv, 0)
    picked = picked_from((0, 1, 3))
    arrived(solg, p4_recv, 1)
    picked = picked + picked_from((2,))
    rows = jnp.where(low, picked[0:256], picked[256:512])
    rows = (rows + swap(rows)).reshape(8, 32, 128)
    pk[...] = jnp.where(low, rows[:, 0:16], rows[:, 16:32]).astype(BF16)
    chg[c] = pk[c]

    def p5(d, to):
        return remote(pk.at[to], chg.at[c], p5_send, p5_recv, 0, "col", to)

    loop(N - 1, lambda n: p5(away(n), lax.rem(c + away(n), N)).start())

    own_rows = picked[512:576]
    out_sol[:, 0] = own_rows[:, 0:64].reshape(8, 8, 64).astype(BF16)
    out_sol[:, 1] = swap(own_rows)[:, 0:64].reshape(8, 8, 64).astype(BF16)

    def sent(n):
        chunk(n // 7, 0, 1, lax.rem(n, 7)).wait_send()

    loop(28, sent)
    all_seven(invg, inv_send)
    for far in (0, 1):
        arrived(msg, p2_send, far)
        arrived(solg, p4_send, far)
    all_seven(redg, p3_send)

    all_seven(chg, p5_recv)
    got = chg[...].reshape(128, 128)
    child = jnp.where(low, dot(s5[0], got), dot(s5[1], got))
    child = child + swap(child)
    out_child[...] = child.T[0:64].astype(BF16)
    all_seven(pk, p5_send)


def on_device(right_side, rest_solution, rest_basis, window_basis, ranks, inverses, child_map):
    any_spec = pl.BlockSpec(memory_space=pl.ANY)
    vmem_spec = pl.BlockSpec(memory_space=pltpu.VMEM)
    dma = pltpu.SemaphoreType.DMA
    sol, child = pl.pallas_call(
        kernel,
        out_shape=(
            pltpu.VMEM((8, 2, 8, 64), BF16),
            pltpu.VMEM((64, 128), BF16),
        ),
        in_specs=[any_spec] * 7,
        out_specs=(vmem_spec, vmem_spec),
        scratch_shapes=[
            pltpu.VMEM((64, 8, 64), BF16),
            pltpu.VMEM((512, 64), F32),
            pltpu.VMEM((64, 8, 64), F32),
            pltpu.VMEM((512, 64), F32),
            pltpu.VMEM((8, 1024, 512), BF16),
            pltpu.VMEM((8, 64, 16, 64), BF16),
            pltpu.VMEM((2, 512), I32),
            pltpu.SMEM((8, 16), I32),
            pltpu.VMEM((4, 8, 64, 128), BF16),
            pltpu.VMEM((4, 1024, 128), F32),
            pltpu.VMEM((16, 256, 128), BF16),
            pltpu.VMEM((16, 128, 256), BF16),
            pltpu.VMEM((16, 256, 128), BF16),
            pltpu.VMEM((8, 64, 128), BF16),
            pltpu.VMEM((8, 64, 128), BF16),
            pltpu.VMEM((64, 128), BF16),
            pltpu.VMEM((8, 64, 128), BF16),
            pltpu.VMEM((8, 2, 8, 512), BF16),
            pltpu.VMEM((128, 512), BF16),
            pltpu.VMEM((8, 64, 128), BF16),
            pltpu.VMEM((576, 512), BF16),
            pltpu.VMEM((2, 128, 128), BF16),
            pltpu.VMEM((8, 16, 128), BF16),
            pltpu.VMEM((8, 16, 128), BF16),
            dma((6,)), dma((8,)), dma((7, 4)), dma((7, 4)),
            dma((1,)), dma((1,)),
            dma((2,)), dma((2,)), dma((1,)), dma((1,)),
            dma((2,)), dma((2,)), dma((1,)), dma((1,)),
        ],
        compiler_params=pltpu.CompilerParams(
            collective_id=0, has_side_effects=True, vmem_limit_bytes=56 * 1024 * 1024
        ),
        cost_estimate=pl.CostEstimate(flops=700_000_000, bytes_accessed=12_000_000, transcendentals=0),
    )(right_side, rest_solution, rest_basis, window_basis, ranks, inverses, child_map)
    solution_rows = sol.reshape(16, 8, 64).transpose(2, 0, 1)
    return solution_rows, child.reshape(64, 2, 64)


def solution(mesh):
    in_specs = (
        P("shot", None, "col"),
        P("shot", "row", "col"),
        P("row", None, None),
        P("row", None, None, "col"),
        P("row", None),
        P(None, ("row", "col"), None),
        P(),
    )
    out_specs = (P("shot", None, ("row", "col")), P("shot", None, ("row", "col")))
    return jax.shard_map(
        on_device, mesh=mesh, in_specs=in_specs, out_specs=out_specs, check_vma=False
    )
```

```python
import jax
import jax.numpy as jnp
from jax import lax
from jax.experimental import pallas as pl
from jax.experimental.pallas import tpu as pltpu
from jax.sharding import PartitionSpec as P

MESH = pl.DeviceIdType.MESH
F32 = jnp.float32
BF16 = jnp.bfloat16
I32 = jnp.int32
N = 8
NEAR = (2, 6, 1, 7)
ROW_ORDER = (4, 5, 2, 3, 6, 7, 1)
FAR_FIRST = (4, 3, 5, 2, 6, 1, 7)


def iota(shape, axis):
    return lax.broadcasted_iota(I32, shape, axis)


def dot(a, b):
    return jnp.dot(a, b, preferred_element_type=F32)


def swap(x):
    return pltpu.roll(x, 64, 1)


def kernel(
    right_ref, sol_ref, basis_ref, wb_ref, ranks_ref, inv_ref, map_ref,
    out_sol, out_child,
    sol_v, sol_f, right_v, right_f, basis_v, wb_v, map_v, ranks_s,
    gath, half, w0, wt, cm, msg, part, red, redg, invg, invl, solg, selm, s5, pk, chg,
    load_sem, basis_sem, ring_send, ring_recv, inv_send, inv_recv,
    p2_send, p2_recv, p3_send, p3_recv, p4_send, p4_recv, p5_send, p5_recv,
):
    r = lax.axis_index("row")
    c = lax.axis_index("col")

    def remote(src, dst, send, recv, at, axis, to):
        return pltpu.make_async_remote_copy(
            src_ref=src, dst_ref=dst, send_sem=send.at[at], recv_sem=recv.at[at],
            device_id={axis: to}, device_id_type=MESH,
        )

    def local(src, dst, sem, at):
        return pltpu.make_async_copy(src, dst, sem.at[at])

    load_sol = local(sol_ref, sol_v, load_sem, 0)
    load_sol.start()
    load_wb = local(wb_ref, wb_v, load_sem, 1)
    load_map = local(
        map_ref.at[:, pl.ds(pl.multiple_of(r * 512, 512), 512)], map_v, load_sem, 2)
    load_ranks = local(ranks_ref, ranks_s, load_sem, 3)
    load_right = local(
        right_ref.at[:, pl.ds(pl.multiple_of((r // 4) * 8, 8), 8), :], right_v, load_sem, 4)
    load_inv = local(
        inv_ref.at[pl.ds(2 * r, 2)], invg.at[r], load_sem, 5)

    barrier = pltpu.get_barrier_semaphore()
    for d in NEAR:
        pl.semaphore_signal(barrier, inc=1, device_id={"col": lax.rem(c + d, N)}, device_id_type=MESH)
    for d in FAR_FIRST:
        pl.semaphore_signal(barrier, inc=1, device_id={"row": lax.rem(r + d, N)}, device_id_type=MESH)

    def loop(count, body):
        def step(n, carry):
            body(n)
            return carry

        lax.fori_loop(0, count, step, 0)

    def all_seven(ref, sem):
        seven = ref.at[pl.ds(0, N - 1)]
        pltpu.make_async_copy(seven, seven, sem.at[0]).wait()

    def row_at(k):
        return lax.rem(r // 2 + k // 2, 4) * 2 + lax.rem(r + k % 2, 2)

    def arrived(ref, sem, far):
        some = ref.at[pl.ds(0, 2 if far else 5)]
        pltpu.make_async_copy(some, some, sem.at[far]).wait()

    def away(n):
        return 4 + (n + 1) // 2 * (1 - 2 * lax.rem(n, 2))

    load_wb.start()
    load_map.start()
    load_ranks.start()
    load_right.start()
    load_inv.start()
    def load_basis(j):
        return local(basis_ref.at[j], basis_v.at[j], basis_sem, j)

    loop(N, lambda j: load_basis(j).start())

    load_sol.wait()
    sol_f[...] = sol_v[...].astype(F32).reshape(512, 64)
    for jj in range(4):
        both = jnp.concatenate(
            [sol_f[pl.ds(2 * jj + h, 64, stride=8), :] for h in range(2)], axis=0)
        gath[jj, c] = both.T.astype(BF16)

    pl.semaphore_wait(barrier, len(NEAR) + len(FAR_FIRST))

    def chunk(jj, slot, to, lane):
        slot, to = lax.rem(c + slot + N, N), lax.rem(c + to + N, N)
        return remote(gath.at[jj, slot], gath.at[jj, slot], ring_send, ring_recv, (lane, jj), "col", to)

    def direct(jj):
        chunk(jj, 0, 2, 0).start()
        chunk(jj, 0, -2, 1).start()

    def next_to(jj):
        chunk(jj, 0, 1, 2).start()
        chunk(jj, 0, -1, 3).start()

    loop(4, direct)
    loop(4, next_to)

    def tile_rows(d, to):
        return remote(inv_ref.at[pl.ds(2 * to, 2)], invg.at[r], inv_send, inv_recv, 0, "row", to)

    loop(N - 1, lambda n: tile_rows(away(n), lax.rem(r + away(n), N)).start())

    def relay(jj):
        way = 1 - 2 * lax.rem(jj, 2)
        for side in (1, -1):
            chunk(jj, -2 * side, 2 * side, (1 - side) // 2).wait_recv()

            @pl.when(way == side)
            def _(side=side):
                chunk(jj, -2 * side, 2 * side, 6).start()

            chunk(jj, -2 * side, side, 4 + (1 - side) // 2).start()

    load_wb.wait()
    row_i, col_i = iota((256, 256), 0), iota((256, 256), 1)
    perm = jnp.where(
        ((row_i >> 4) == (col_i & 15)) & ((row_i & 15) == (col_i >> 4)), 1.0, 0.0).astype(BF16)

    def regroup(step):
        jj, kb = step // 4, lax.rem(step, 4)
        k0 = pl.multiple_of(kb * 16, 16)
        x = jnp.concatenate(
            [wb_v[2 * jj + h, pl.ds(k0, 16)].reshape(256, 64) for h in range(2)], axis=1)
        y = dot(perm, x).astype(BF16).reshape(16, 16, 128)
        w0[:, pl.ds(pl.multiple_of(jj * 64 + kb * 16, 16), 16), :] = y

    def regroups(n):
        for k in range(4):
            regroup(4 * n + k)

    loop(4, regroups)

    def turn(i):
        wt[i] = w0[i].T

    def turns(n):
        for k in range(4):
            turn(4 * n + k)

    loop(4, turns)
    loop(4, relay)

    low = iota((1, 128), 1) < 64

    def coeffs(jj, first):
        pairs = [lax.rem(first + k, 4) for k in range(2)]
        g = jnp.concatenate([gath[jj, pl.ds(2 * p, 2)].reshape(128, 128) for p in pairs], axis=0)
        both = []
        for h in range(2):
            cols = [pl.ds(pl.multiple_of(p * 128, 128), 128) for p in pairs]
            both.append(dot(jnp.concatenate([basis_v[2 * jj + h, :, at] for at in cols], axis=1), g))
        return jnp.where(low, both[0], both[1])

    near = lax.rem((c + 7) // 2, 4)

    def near_half(jj):
        chunk(jj, 0, 1, 2).wait_recv()
        chunk(jj, 0, 1, 3).wait_recv()
        load_basis(2 * jj).wait()
        load_basis(2 * jj + 1).wait()
        half[jj] = coeffs(jj, near)

    loop(4, near_half)

    load_ranks.wait()
    k_of = iota((64, 128), 0)

    def far_half(jj):
        for lane in (4, 5, 6):
            chunk(jj, 0, 1, lane).wait_recv()
        total = half[jj] + coeffs(jj, lax.rem(near + 2, 4))
        for i in range(16):
            limit = jnp.where(low, ranks_s[2 * jj, i], ranks_s[2 * jj + 1, i])
            cut = jnp.where(k_of < limit, total[i * 64:(i + 1) * 64], 0.0)
            cm[i, pl.ds(pl.multiple_of(jj * 64, 64), 64), :] = cut.astype(BF16)

    loop(4, far_half)

    def update(to):
        sums = []
        for h in range(2):
            u = dot(wt[2 * to + h], cm[2 * to + h])
            sums.append(jnp.where(low, u[0:64], u[64:128]))
        return jnp.where(low, sums[0], sums[1]) + swap(jnp.where(low, sums[1], sums[0]))

    def p2(d, to):
        return remote(msg.at[d], part.at[d], p2_send, p2_recv, int(d // 2 == 2), "row", to)

    for k in ROW_ORDER:
        msg[k] = update(row_at(k)).astype(BF16)
        p2(k, row_at(k)).start()
    own_update = update(r)

    load_map.wait()
    w = map_v[...]
    cc = (w >> 3) & 7
    code = (((w >> 9) & 1) << 9) + ((w >> 10) << 6) + (((w >> 6) & 7) << 3) + (w & 7) + 1
    mine = cc == c
    mine_f = jnp.where(mine, 1.0, 0.0)
    mine8 = jnp.where(iota((8, 512), 0) == 0, mine_f[0:1], mine_f[1:2]).astype(BF16)
    ta, tb = iota((512, 512), 0), iota((512, 512), 1)
    same = (ta >> 6) == (tb >> 6)
    before = dot(mine8, jnp.where(same & (ta < tb), 1.0, 0.0).astype(BF16))
    total = dot(mine8, jnp.where(same, 1.0, 0.0).astype(BF16))
    place = (before[0:1].astype(I32), (before[1:2] + total[0:1]).astype(I32))
    code_f = jnp.where(mine, code, 0).astype(F32)
    slots = []
    for g in range(4):
        at = slice(g * 128, (g + 1) * 128)
        ra, la = iota((64, 128), 0), iota((64, 128), 1)
        ours = (ra >> 5) == (la >> 6)
        acc = jnp.zeros((64, 128), F32)
        for ch in range(2):
            take = ours & ((ra & 31) == place[ch][:, at])
            acc = acc + jnp.where(take, code_f[ch:ch + 1, at], 0.0)
        slots.append(jnp.sum(acc, axis=1, keepdims=True))
    slot = jnp.concatenate(slots, axis=0).astype(I32)
    src = iota((256, 512), 1) + 1
    for h in range(2):
        selm[h * 256:(h + 1) * 256, :] = jnp.where(src + h * 512 == slot, 1.0, 0.0).astype(BF16)
    ra, la = iota((64, 512), 0), iota((64, 512), 1)
    selm[512:576, :] = jnp.where(
        la == ((ra >> 3) << 6) + r * 8 + (ra & 7), 1.0, 0.0).astype(BF16)

    load_right.wait()
    right_f[...] = right_v[...].reshape(512, 64)
    base = 2 * lax.rem(r, 4)
    right_t = jnp.concatenate(
        [right_f[pl.ds(base + h, 64, stride=8), :] for h in range(2)], axis=0).T

    acc = right_t - own_update
    for far in (0, 1):
        arrived(part, p2_recv, far)
        for k in ROW_ORDER:
            if int(k // 2 == 2) == far:
                acc = acc - part[k].astype(F32)
    red[...] = acc.astype(BF16)
    redg[c] = acc.astype(BF16)

    def p3(d, to):
        return remote(red, redg.at[c], p3_send, p3_recv, int(d in (3, 4, 5)), "col", to)

    for d in FAR_FIRST:
        p3(d, lax.rem(c + d, N)).start()
    load_inv.wait()
    all_seven(invg, inv_recv)
    for h in range(2):
        invl[h * 64:(h + 1) * 64, :] = invg[:, h].astype(F32).reshape(64, 512).astype(BF16)

    x = map_v[:, pl.ds(pl.multiple_of((c // 2) * 128, 128), 128)]
    x_swapped = swap(x)
    odd = lax.rem(c, 2) == 1
    own = jnp.where(
        low, jnp.where(odd, x_swapped[0:1], x[0:1]), jnp.where(odd, x[1:2], x_swapped[1:2]))
    class_l = ((own >> 3) & 7).astype(F32)
    qa, qb = iota((128, 128), 0), iota((128, 128), 1)
    class_s = jnp.sum(jnp.where(qa == qb, class_l, 0.0), axis=1, keepdims=True)
    rank_s = jnp.sum(jnp.where((class_s == class_l) & (qb < qa), 1.0, 0.0), axis=1, keepdims=True)
    rank_i = rank_s.astype(I32)
    found = class_s.astype(I32) * 16 + (rank_i & 15)
    for h in range(2):
        s5[h] = jnp.where((qb == found) & ((rank_i >> 4) == h), 1.0, 0.0).astype(BF16)


    s = 0.0
    for far in (0, 1):
        some = redg.at[pl.ds(0, 3 if far else 4)]
        pltpu.make_async_copy(some, some, p3_recv.at[far]).wait()
        at = [lax.rem(near + 2 * far + k, 4) for k in range(2)]
        tiles = jnp.concatenate([invl[:, pl.ds(pl.multiple_of(p * 128, 128), 128)] for p in at], axis=1)
        s = s + dot(tiles, jnp.concatenate([redg[pl.ds(2 * p, 2)].reshape(128, 128) for p in at], axis=0))
    solved = jnp.where(low, s[0:64], s[64:128]).astype(BF16)
    solg[r] = solved

    def p4(d, to):
        return remote(solg.at[r], solg.at[r], p4_send, p4_recv, int(d // 2 == 2), "row", to)

    for k in ROW_ORDER:
        p4(k, row_at(k)).start()

    def picked_from(chips):
        at = [lax.rem(r // 2 + k, 4) for k in chips]
        table = jnp.concatenate([selm[:, pl.ds(pl.multiple_of(p * 128, 128), 128)] for p in at], axis=1)
        rows = jnp.concatenate([solg[pl.ds(2 * p, 2)].reshape(128, 128) for p in at], axis=0)
        return dot(table, rows)

    arrived(solg, p4_recv, 0)
    picked = picked_from((0, 1, 3))
    arrived(solg, p4_recv, 1)
    picked = picked + picked_from((2,))
    rows = jnp.where(low, picked[0:256], picked[256:512])
    rows = (rows + swap(rows)).reshape(8, 32, 128)
    pk[...] = jnp.where(low, rows[:, 0:16], rows[:, 16:32]).astype(BF16)
    chg[c] = pk[c]

    def p5(d, to):
        return remote(pk.at[to], chg.at[c], p5_send, p5_recv, 0, "col", to)

    loop(N - 1, lambda n: p5(away(n), lax.rem(c + away(n), N)).start())

    own_rows = picked[512:576]
    out_sol[:, 0] = own_rows[:, 0:64].reshape(8, 8, 64).astype(BF16)
    out_sol[:, 1] = swap(own_rows)[:, 0:64].reshape(8, 8, 64).astype(BF16)

    def sent(n):
        chunk(n // 7, 0, 1, lax.rem(n, 7)).wait_send()

    loop(28, sent)
    all_seven(invg, inv_send)
    for far in (0, 1):
        arrived(msg, p2_send, far)
        arrived(solg, p4_send, far)
    for far in (0, 1):
        some = redg.at[pl.ds(0, 3 if far else 4)]
        pltpu.make_async_copy(some, some, p3_send.at[far]).wait()

    all_seven(chg, p5_recv)
    got = chg[...].reshape(128, 128)
    child = jnp.where(low, dot(s5[0], got), dot(s5[1], got))
    child = child + swap(child)
    out_child[...] = child.T[0:64].astype(BF16)
    all_seven(pk, p5_send)


def on_device(right_side, rest_solution, rest_basis, window_basis, ranks, inverses, child_map):
    any_spec = pl.BlockSpec(memory_space=pl.ANY)
    vmem_spec = pl.BlockSpec(memory_space=pltpu.VMEM)
    dma = pltpu.SemaphoreType.DMA
    sol, child = pl.pallas_call(
        kernel,
        out_shape=(
            pltpu.VMEM((8, 2, 8, 64), BF16),
            pltpu.VMEM((64, 128), BF16),
        ),
        in_specs=[any_spec] * 7,
        out_specs=(vmem_spec, vmem_spec),
        scratch_shapes=[
            pltpu.VMEM((64, 8, 64), BF16),
            pltpu.VMEM((512, 64), F32),
            pltpu.VMEM((64, 8, 64), F32),
            pltpu.VMEM((512, 64), F32),
            pltpu.VMEM((8, 1024, 512), BF16),
            pltpu.VMEM((8, 64, 16, 64), BF16),
            pltpu.VMEM((2, 512), I32),
            pltpu.SMEM((8, 16), I32),
            pltpu.VMEM((4, 8, 64, 128), BF16),
            pltpu.VMEM((4, 1024, 128), F32),
            pltpu.VMEM((16, 256, 128), BF16),
            pltpu.VMEM((16, 128, 256), BF16),
            pltpu.VMEM((16, 256, 128), BF16),
            pltpu.VMEM((8, 64, 128), BF16),
            pltpu.VMEM((8, 64, 128), BF16),
            pltpu.VMEM((64, 128), BF16),
            pltpu.VMEM((8, 64, 128), BF16),
            pltpu.VMEM((8, 2, 8, 512), BF16),
            pltpu.VMEM((128, 512), BF16),
            pltpu.VMEM((8, 64, 128), BF16),
            pltpu.VMEM((576, 512), BF16),
            pltpu.VMEM((2, 128, 128), BF16),
            pltpu.VMEM((8, 16, 128), BF16),
            pltpu.VMEM((8, 16, 128), BF16),
            dma((6,)), dma((8,)), dma((7, 4)), dma((7, 4)),
            dma((1,)), dma((1,)),
            dma((2,)), dma((2,)), dma((2,)), dma((2,)),
            dma((2,)), dma((2,)), dma((1,)), dma((1,)),
        ],
        compiler_params=pltpu.CompilerParams(
            collective_id=0, has_side_effects=True, vmem_limit_bytes=56 * 1024 * 1024
        ),
        cost_estimate=pl.CostEstimate(flops=700_000_000, bytes_accessed=12_000_000, transcendentals=0),
    )(right_side, rest_solution, rest_basis, window_basis, ranks, inverses, child_map)
    solution_rows = sol.reshape(16, 8, 64).transpose(2, 0, 1)
    return solution_rows, child.reshape(64, 2, 64)


def solution(mesh):
    in_specs = (
        P("shot", None, "col"),
        P("shot", "row", "col"),
        P("row", None, None),
        P("row", None, None, "col"),
        P("row", None),
        P(None, ("row", "col"), None),
        P(),
    )
    out_specs = (P("shot", None, ("row", "col")), P("shot", None, ("row", "col")))
    return jax.shard_map(
        on_device, mesh=mesh, in_specs=in_specs, out_specs=out_specs, check_vma=False
    )
```

```python
import jax
import jax.numpy as jnp
from jax import lax
from jax.experimental import pallas as pl
from jax.experimental.pallas import tpu as pltpu
from jax.sharding import PartitionSpec as P

MESH = pl.DeviceIdType.MESH
F32 = jnp.float32
BF16 = jnp.bfloat16
I32 = jnp.int32
N = 8
NEAR = (2, 6, 1, 7)
ROW_ORDER = (4, 5, 2, 3, 6, 7, 1)
FAR_FIRST = (4, 3, 5, 2, 6, 1, 7)


def iota(shape, axis):
    return lax.broadcasted_iota(I32, shape, axis)


def dot(a, b):
    return jnp.dot(a, b, preferred_element_type=F32)


def swap(x):
    return pltpu.roll(x, 64, 1)


def kernel(
    right_ref, sol_ref, basis_ref, wb_ref, ranks_ref, inv_ref, map_ref,
    out_sol, out_child,
    sol_v, sol_f, right_v, right_f, basis_v, wb_v, map_v, ranks_s,
    gath, half, w0, wt, cm, msg, part, red, redg, invg, invl, solg, selm, s5, pk, chg,
    load_sem, basis_sem, ring_send, ring_recv, inv_send, inv_recv,
    p2_send, p2_recv, p3_send, p3_recv, p4_send, p4_recv, p5_send, p5_recv,
):
    r = lax.axis_index("row")
    c = lax.axis_index("col")

    def remote(src, dst, send, recv, at, axis, to):
        return pltpu.make_async_remote_copy(
            src_ref=src, dst_ref=dst, send_sem=send.at[at], recv_sem=recv.at[at],
            device_id={axis: to}, device_id_type=MESH,
        )

    def local(src, dst, sem, at):
        return pltpu.make_async_copy(src, dst, sem.at[at])

    load_sol = local(sol_ref, sol_v, load_sem, 0)
    load_sol.start()
    load_wb = local(wb_ref, wb_v, load_sem, 1)
    load_map = local(
        map_ref.at[:, pl.ds(pl.multiple_of(r * 512, 512), 512)], map_v, load_sem, 2)
    load_ranks = local(ranks_ref, ranks_s, load_sem, 3)
    load_right = local(
        right_ref.at[:, pl.ds(pl.multiple_of((r // 4) * 8, 8), 8), :], right_v, load_sem, 4)
    load_inv = local(
        inv_ref.at[pl.ds(2 * r, 2)], invg.at[r], load_sem, 5)

    barrier = pltpu.get_barrier_semaphore()
    for d in NEAR:
        pl.semaphore_signal(barrier, inc=1, device_id={"col": lax.rem(c + d, N)}, device_id_type=MESH)
    for d in FAR_FIRST:
        pl.semaphore_signal(barrier, inc=1, device_id={"row": lax.rem(r + d, N)}, device_id_type=MESH)

    def loop(count, body):
        def step(n, carry):
            body(n)
            return carry

        lax.fori_loop(0, count, step, 0)

    def all_seven(ref, sem):
        seven = ref.at[pl.ds(0, N - 1)]
        pltpu.make_async_copy(seven, seven, sem.at[0]).wait()

    def row_at(k):
        return lax.rem(r // 2 + k // 2, 4) * 2 + lax.rem(r + k % 2, 2)

    def arrived(ref, sem, far):
        some = ref.at[pl.ds(0, 2 if far else 5)]
        pltpu.make_async_copy(some, some, sem.at[far]).wait()

    def away(n):
        return 4 + (n + 1) // 2 * (1 - 2 * lax.rem(n, 2))

    load_wb.start()
    load_map.start()
    load_ranks.start()
    load_right.start()
    load_inv.start()
    def load_basis(j):
        return local(basis_ref.at[j], basis_v.at[j], basis_sem, j)

    loop(N, lambda j: load_basis(j).start())

    load_sol.wait()
    sol_f[...] = sol_v[...].astype(F32).reshape(512, 64)
    for jj in range(4):
        both = jnp.concatenate(
            [sol_f[pl.ds(2 * jj + h, 64, stride=8), :] for h in range(2)], axis=0)
        gath[jj, c] = both.T.astype(BF16)

    pl.semaphore_wait(barrier, len(NEAR) + len(FAR_FIRST))

    def chunk(jj, slot, to, lane):
        slot, to = lax.rem(c + slot + N, N), lax.rem(c + to + N, N)
        return remote(gath.at[jj, slot], gath.at[jj, slot], ring_send, ring_recv, (lane, jj), "col", to)

    def direct(jj):
        chunk(jj, 0, 2, 0).start()
        chunk(jj, 0, -2, 1).start()

    def next_to(jj):
        chunk(jj, 0, 1, 2).start()
        chunk(jj, 0, -1, 3).start()

    loop(4, direct)
    loop(4, next_to)

    def tile_rows(d, to):
        return remote(inv_ref.at[pl.ds(2 * to, 2)], invg.at[r], inv_send, inv_recv, 0, "row", to)

    loop(N - 1, lambda n: tile_rows(away(n), lax.rem(r + away(n), N)).start())

    def relay(jj):
        way = 1 - 2 * lax.rem(jj, 2)
        for side in (1, -1):
            chunk(jj, -2 * side, 2 * side, (1 - side) // 2).wait_recv()

            @pl.when(way == side)
            def _(side=side):
                chunk(jj, -2 * side, 2 * side, 6).start()

            chunk(jj, -2 * side, side, 4 + (1 - side) // 2).start()

    load_wb.wait()
    row_i, col_i = iota((256, 256), 0), iota((256, 256), 1)
    perm = jnp.where(
        ((row_i >> 4) == (col_i & 15)) & ((row_i & 15) == (col_i >> 4)), 1.0, 0.0).astype(BF16)

    def regroup(step):
        jj, kb = step // 4, lax.rem(step, 4)
        k0 = pl.multiple_of(kb * 16, 16)
        x = jnp.concatenate(
            [wb_v[2 * jj + h, pl.ds(k0, 16)].reshape(256, 64) for h in range(2)], axis=1)
        y = dot(perm, x).astype(BF16).reshape(16, 16, 128)
        w0[:, pl.ds(pl.multiple_of(jj * 64 + kb * 16, 16), 16), :] = y

    def regroups(n):
        for k in range(4):
            regroup(4 * n + k)

    loop(4, regroups)

    def turn(i):
        wt[i] = w0[i].T

    def turns(n):
        for k in range(4):
            turn(4 * n + k)

    loop(4, turns)
    loop(4, relay)

    low = iota((1, 128), 1) < 64

    def coeffs(jj, first):
        pairs = [lax.rem(first + k, 4) for k in range(2)]
        g = jnp.concatenate([gath[jj, pl.ds(2 * p, 2)].reshape(128, 128) for p in pairs], axis=0)
        both = []
        for h in range(2):
            cols = [pl.ds(pl.multiple_of(p * 128, 128), 128) for p in pairs]
            both.append(dot(jnp.concatenate([basis_v[2 * jj + h, :, at] for at in cols], axis=1), g))
        return jnp.where(low, both[0], both[1])

    near = lax.rem((c + 7) // 2, 4)

    def near_half(jj):
        chunk(jj, 0, 1, 2).wait_recv()
        chunk(jj, 0, 1, 3).wait_recv()
        load_basis(2 * jj).wait()
        load_basis(2 * jj + 1).wait()
        half[jj] = coeffs(jj, near)

    loop(4, near_half)

    load_ranks.wait()
    k_of = iota((64, 128), 0)

    def far_half(jj):
        for lane in (4, 5, 6):
            chunk(jj, 0, 1, lane).wait_recv()
        total = half[jj] + coeffs(jj, lax.rem(near + 2, 4))
        for i in range(16):
            limit = jnp.where(low, ranks_s[2 * jj, i], ranks_s[2 * jj + 1, i])
            cut = jnp.where(k_of < limit, total[i * 64:(i + 1) * 64], 0.0)
            cm[i, pl.ds(pl.multiple_of(jj * 64, 64), 64), :] = cut.astype(BF16)

    loop(4, far_half)

    def update(to):
        sums = []
        for h in range(2):
            u = dot(wt[2 * to + h], cm[2 * to + h])
            sums.append(jnp.where(low, u[0:64], u[64:128]))
        return jnp.where(low, sums[0], sums[1]) + swap(jnp.where(low, sums[1], sums[0]))

    def p2(d, to):
        return remote(msg.at[d], part.at[d], p2_send, p2_recv, int(d // 2 == 2), "row", to)

    for k in ROW_ORDER:
        msg[k] = update(row_at(k)).astype(BF16)
        p2(k, row_at(k)).start()
    own_update = update(r)

    load_right.wait()
    right_f[...] = right_v[...].reshape(512, 64)
    base = 2 * lax.rem(r, 4)
    right_t = jnp.concatenate(
        [right_f[pl.ds(base + h, 64, stride=8), :] for h in range(2)], axis=0).T

    acc = right_t - own_update
    for far in (0, 1):
        arrived(part, p2_recv, far)
        for k in ROW_ORDER:
            if int(k // 2 == 2) == far:
                acc = acc - part[k].astype(F32)
    red[...] = acc.astype(BF16)
    redg[c] = acc.astype(BF16)

    def p3(d, to):
        return remote(red, redg.at[c], p3_send, p3_recv, int(d in (3, 4, 5)), "col", to)

    for d in FAR_FIRST:
        p3(d, lax.rem(c + d, N)).start()
    load_inv.wait()
    all_seven(invg, inv_recv)
    for h in range(2):
        invl[h * 64:(h + 1) * 64, :] = invg[:, h].astype(F32).reshape(64, 512).astype(BF16)

    load_map.wait()
    w = map_v[...]
    cc = (w >> 3) & 7
    code = (((w >> 9) & 1) << 9) + ((w >> 10) << 6) + (((w >> 6) & 7) << 3) + (w & 7) + 1
    mine = cc == c
    mine_f = jnp.where(mine, 1.0, 0.0)
    mine8 = jnp.where(iota((8, 512), 0) == 0, mine_f[0:1], mine_f[1:2]).astype(BF16)
    ta, tb = iota((512, 512), 0), iota((512, 512), 1)
    same = (ta >> 6) == (tb >> 6)
    before = dot(mine8, jnp.where(same & (ta < tb), 1.0, 0.0).astype(BF16))
    total = dot(mine8, jnp.where(same, 1.0, 0.0).astype(BF16))
    place = (before[0:1].astype(I32), (before[1:2] + total[0:1]).astype(I32))
    code_f = jnp.where(mine, code, 0).astype(F32)
    slots = []
    for g in range(4):
        at = slice(g * 128, (g + 1) * 128)
        ra, la = iota((64, 128), 0), iota((64, 128), 1)
        ours = (ra >> 5) == (la >> 6)
        acc = jnp.zeros((64, 128), F32)
        for ch in range(2):
            take = ours & ((ra & 31) == place[ch][:, at])
            acc = acc + jnp.where(take, code_f[ch:ch + 1, at], 0.0)
        slots.append(jnp.sum(acc, axis=1, keepdims=True))
    slot = jnp.concatenate(slots, axis=0).astype(I32)
    src = iota((256, 512), 1) + 1
    for h in range(2):
        selm[h * 256:(h + 1) * 256, :] = jnp.where(src + h * 512 == slot, 1.0, 0.0).astype(BF16)
    ra, la = iota((64, 512), 0), iota((64, 512), 1)
    selm[512:576, :] = jnp.where(
        la == ((ra >> 3) << 6) + r * 8 + (ra & 7), 1.0, 0.0).astype(BF16)

    x = map_v[:, pl.ds(pl.multiple_of((c // 2) * 128, 128), 128)]
    x_swapped = swap(x)
    odd = lax.rem(c, 2) == 1
    own = jnp.where(
        low, jnp.where(odd, x_swapped[0:1], x[0:1]), jnp.where(odd, x[1:2], x_swapped[1:2]))
    class_l = ((own >> 3) & 7).astype(F32)
    qa, qb = iota((128, 128), 0), iota((128, 128), 1)
    class_s = jnp.sum(jnp.where(qa == qb, class_l, 0.0), axis=1, keepdims=True)
    rank_s = jnp.sum(jnp.where((class_s == class_l) & (qb < qa), 1.0, 0.0), axis=1, keepdims=True)
    rank_i = rank_s.astype(I32)
    found = class_s.astype(I32) * 16 + (rank_i & 15)
    for h in range(2):
        s5[h] = jnp.where((qb == found) & ((rank_i >> 4) == h), 1.0, 0.0).astype(BF16)


    s = 0.0
    for far in (0, 1):
        some = redg.at[pl.ds(0, 3 if far else 4)]
        pltpu.make_async_copy(some, some, p3_recv.at[far]).wait()
        at = [lax.rem(near + 2 * far + k, 4) for k in range(2)]
        tiles = jnp.concatenate([invl[:, pl.ds(pl.multiple_of(p * 128, 128), 128)] for p in at], axis=1)
        s = s + dot(tiles, jnp.concatenate([redg[pl.ds(2 * p, 2)].reshape(128, 128) for p in at], axis=0))
    solved = jnp.where(low, s[0:64], s[64:128]).astype(BF16)
    solg[r] = solved

    def p4(d, to):
        return remote(solg.at[r], solg.at[r], p4_send, p4_recv, int(d // 2 == 2), "row", to)

    for k in ROW_ORDER:
        p4(k, row_at(k)).start()

    def picked_from(chips):
        at = [lax.rem(r // 2 + k, 4) for k in chips]
        table = jnp.concatenate([selm[:, pl.ds(pl.multiple_of(p * 128, 128), 128)] for p in at], axis=1)
        rows = jnp.concatenate([solg[pl.ds(2 * p, 2)].reshape(128, 128) for p in at], axis=0)
        return dot(table, rows)

    arrived(solg, p4_recv, 0)
    picked = picked_from((0, 1, 3))
    arrived(solg, p4_recv, 1)
    picked = picked + picked_from((2,))
    rows = jnp.where(low, picked[0:256], picked[256:512])
    rows = (rows + swap(rows)).reshape(8, 32, 128)
    pk[...] = jnp.where(low, rows[:, 0:16], rows[:, 16:32]).astype(BF16)
    chg[c] = pk[c]

    def p5(d, to):
        return remote(pk.at[to], chg.at[c], p5_send, p5_recv, 0, "col", to)

    loop(N - 1, lambda n: p5(away(n), lax.rem(c + away(n), N)).start())

    own_rows = picked[512:576]
    out_sol[:, 0] = own_rows[:, 0:64].reshape(8, 8, 64).astype(BF16)
    out_sol[:, 1] = swap(own_rows)[:, 0:64].reshape(8, 8, 64).astype(BF16)

    def sent(n):
        chunk(n // 7, 0, 1, lax.rem(n, 7)).wait_send()

    loop(28, sent)
    all_seven(invg, inv_send)
    for far in (0, 1):
        arrived(msg, p2_send, far)
        arrived(solg, p4_send, far)
    for far in (0, 1):
        some = redg.at[pl.ds(0, 3 if far else 4)]
        pltpu.make_async_copy(some, some, p3_send.at[far]).wait()

    all_seven(chg, p5_recv)
    got = chg[...].reshape(128, 128)
    child = jnp.where(low, dot(s5[0], got), dot(s5[1], got))
    child = child + swap(child)
    out_child[...] = child.T[0:64].astype(BF16)
    all_seven(pk, p5_send)


def on_device(right_side, rest_solution, rest_basis, window_basis, ranks, inverses, child_map):
    any_spec = pl.BlockSpec(memory_space=pl.ANY)
    vmem_spec = pl.BlockSpec(memory_space=pltpu.VMEM)
    dma = pltpu.SemaphoreType.DMA
    sol, child = pl.pallas_call(
        kernel,
        out_shape=(
            pltpu.VMEM((8, 2, 8, 64), BF16),
            pltpu.VMEM((64, 128), BF16),
        ),
        in_specs=[any_spec] * 7,
        out_specs=(vmem_spec, vmem_spec),
        scratch_shapes=[
            pltpu.VMEM((64, 8, 64), BF16),
            pltpu.VMEM((512, 64), F32),
            pltpu.VMEM((64, 8, 64), F32),
            pltpu.VMEM((512, 64), F32),
            pltpu.VMEM((8, 1024, 512), BF16),
            pltpu.VMEM((8, 64, 16, 64), BF16),
            pltpu.VMEM((2, 512), I32),
            pltpu.SMEM((8, 16), I32),
            pltpu.VMEM((4, 8, 64, 128), BF16),
            pltpu.VMEM((4, 1024, 128), F32),
            pltpu.VMEM((16, 256, 128), BF16),
            pltpu.VMEM((16, 128, 256), BF16),
            pltpu.VMEM((16, 256, 128), BF16),
            pltpu.VMEM((8, 64, 128), BF16),
            pltpu.VMEM((8, 64, 128), BF16),
            pltpu.VMEM((64, 128), BF16),
            pltpu.VMEM((8, 64, 128), BF16),
            pltpu.VMEM((8, 2, 8, 512), BF16),
            pltpu.VMEM((128, 512), BF16),
            pltpu.VMEM((8, 64, 128), BF16),
            pltpu.VMEM((576, 512), BF16),
            pltpu.VMEM((2, 128, 128), BF16),
            pltpu.VMEM((8, 16, 128), BF16),
            pltpu.VMEM((8, 16, 128), BF16),
            dma((6,)), dma((8,)), dma((7, 4)), dma((7, 4)),
            dma((1,)), dma((1,)),
            dma((2,)), dma((2,)), dma((2,)), dma((2,)),
            dma((2,)), dma((2,)), dma((1,)), dma((1,)),
        ],
        compiler_params=pltpu.CompilerParams(
            collective_id=0, has_side_effects=True, vmem_limit_bytes=56 * 1024 * 1024
        ),
        cost_estimate=pl.CostEstimate(flops=700_000_000, bytes_accessed=12_000_000, transcendentals=0),
    )(right_side, rest_solution, rest_basis, window_basis, ranks, inverses, child_map)
    solution_rows = sol.reshape(16, 8, 64).transpose(2, 0, 1)
    return solution_rows, child.reshape(64, 2, 64)


def solution(mesh):
    in_specs = (
        P("shot", None, "col"),
        P("shot", "row", "col"),
        P("row", None, None),
        P("row", None, None, "col"),
        P("row", None),
        P(None, ("row", "col"), None),
        P(),
    )
    out_specs = (P("shot", None, ("row", "col")), P("shot", None, ("row", "col")))
    return jax.shard_map(
        on_device, mesh=mesh, in_specs=in_specs, out_specs=out_specs, check_vma=False
    )
```
